128 devices in a mesh: snap: 8 (over z_lo, y), height: 16 (over z_hi, x, core).
Axes of the slice: x: 4, y: 4, z: 4 (z_hi: 2, z_lo: 2; z = z_hi * 2 + z_lo), core: 2. Of those that a mesh axis runs over, the one named last changes fastest.
Arguments:
- resolved: bfloat16 [128, 3, 128, 16, 2, 128], P('snap', None, 'height'), may hold values from -6 to 6
- drain: bfloat16 [128, 3, 128, 16, 2, 128], P('snap', None, 'height'), may hold values from -6 to 6
- pair_list: int32 [256, 2], replicated, may hold values from 0 to 127, as said below
- ridge_index: int32 [256], replicated, may hold values from 0 to 3
Outputs:
- predicted: float32 [128, 3, 128, 2, 256], P('snap', None, 'height')
- misfit: float32 [1], replicated
The draws below stay inside these ranges and needn't reach their ends.
Inputs may be any that keep to these rules, and one draw needn't show every extreme that they name: `pair_list`: each row names a streamwise mode below 16 and a spanwise wavenumber below 128; no row repeats.
All inputs are finite; a program needn't handle non-finite values.
Results may differ from the reference program's by a relative error of at most 0.0032.
Values sent between devices are 32-bit elements; how exact they have to be, the bound alone decides.
No kernel may reach another device: no remote copies, remote signals or barrier semaphores. Data moves between devices by JAX's collectives and lax.ppermute only.
A program may use at most 128 MiB of HBM per device.

```python
import math
import jax
import jax.numpy as jnp
from jax import lax

Z = 128
KX = 16
H = 128
C = 3
S = 128
PAIRS = 256


def draw_pair_list(key, part):
    total = KX * Z
    first = jax.random.permutation(jax.random.fold_in(key, 11), total - 1)[:PAIRS - 1].astype(jnp.int32)
    chosen = jnp.concatenate([first, jnp.full((1,), total - 1, jnp.int32)])
    order = jax.random.permutation(jax.random.fold_in(key, 12), PAIRS)
    chosen = chosen[order]
    return jnp.stack([chosen // Z, chosen % Z], axis=1).astype(jnp.int32)


def plant(entries, stream_key, least, high):
    place = [jax.random.randint(jax.random.fold_in(stream_key, axis), (), 0, length) for axis, length in enumerate(entries.shape)]
    longest = entries.shape.index(max(entries.shape))
    neighbour = place[:longest] + [(place[longest] + 1) % entries.shape[longest]] + place[longest + 1:]
    return entries.at[tuple(place)].set(least).at[tuple(neighbour)].set(high)


def shard_levels(rng, dims, shards, least, largest):
    def one(position, parts):
        heights = jax.random.uniform(jax.random.fold_in(jax.random.fold_in(rng, 6), position), (parts,), jnp.float32, least / len(shards), largest / len(shards))
        return jnp.repeat(jnp.exp(heights), dims[position] // parts).reshape((-1,) + (1,) * (len(dims) - position - 1))

    level = one(*shards[0])
    for cut in shards[1:]:
        level = level * one(*cut)
    return level


def bell_draw(stream_key, extent, scale, limit, split=(), held_as=jnp.bfloat16):
    level = shard_levels(stream_key, extent, split, -0.22, 0.18) if split else 1.0
    drawn = jax.random.normal(stream_key, extent, jnp.float32) * scale * level
    return jnp.minimum(jnp.maximum(drawn, -limit), limit).astype(held_as)


def setup_inputs(seed: int = 0) -> dict:
    keys = jax.random.split(jax.random.key(seed), 5)
    return {
        "resolved": bell_draw(keys[0], (S, C, H, KX, 2, Z), 1.0, 6.0, ((0, 8), (2, 16))),
        "drain": bell_draw(keys[1], (S, C, H, KX, 2, Z), 1.0, 6.0, ((0, 8), (2, 16))),
        "pair_list": draw_pair_list(jax.random.fold_in(keys[4], 71), 0),
        "ridge_index": plant(jax.random.randint(keys[3], (PAIRS,), 0, 4), jax.random.fold_in(keys[3], 1), 0, 3).astype(jnp.int32),
    }


def twiddles(length):
    grid = jnp.arange(length, dtype=jnp.int32)
    phase = grid[:, None] * grid[None, :] % length
    theta = phase.astype(jnp.float32) * (2.0 * math.pi / length)
    scaling = 1.0 / math.sqrt(length)
    cosine = jnp.cos(theta) * scaling
    sine = jnp.sin(theta) * scaling
    upper = jnp.concatenate([cosine, -sine], axis=1)
    lower = jnp.concatenate([sine, cosine], axis=1)
    return jnp.concatenate([upper, lower], axis=0).astype(jnp.bfloat16)

def spectrum_at(values, entry, twiddle):
    mode_rows = jnp.take(values, entry[0], axis=3)
    picked = jnp.stack([jnp.take(twiddle, entry[1], axis=1), jnp.take(twiddle, entry[1] + Z, axis=1)], axis=1)
    spectral = jnp.dot(mode_rows.reshape(-1, 2 * Z).astype(jnp.float32), picked.astype(jnp.float32), preferred_element_type=jnp.float32)
    return spectral.reshape(S, C * H, 2)

def reference(resolved, drain, pair_list, ridge_index):
    twiddle = twiddles(Z)
    features = C * H
    identity_matrix = jnp.eye(2 * features, dtype=jnp.float32)
    highest = lax.Precision.HIGHEST

    def one_pair(packed):
        entry, level = packed
        ridge = 0.25 * jnp.exp2(level.astype(jnp.float32))
        spec_x = spectrum_at(resolved, entry, twiddle)
        spec_y = spectrum_at(drain, entry, twiddle)
        real_x = spec_x[:, :, 0]
        imag_x = spec_x[:, :, 1]
        stacked_x = jnp.concatenate([jnp.concatenate([real_x, imag_x], 1), jnp.concatenate([-imag_x, real_x], 1)], 0)
        stacked_y = jnp.concatenate([spec_y[:, :, 0], spec_y[:, :, 1]], 0)
        gram = jnp.dot(stacked_x.T.astype(jnp.float32), stacked_x.astype(jnp.float32), precision=highest, preferred_element_type=jnp.float32) / S + ridge * identity_matrix
        moments = jnp.dot(stacked_x.T.astype(jnp.float32), stacked_y.astype(jnp.float32), precision=highest, preferred_element_type=jnp.float32) / S
        factor = jnp.linalg.cholesky(gram)
        halfway = lax.linalg.triangular_solve(factor, moments, left_side=True, lower=True, transpose_a=False)
        weights = lax.linalg.triangular_solve(factor, halfway, left_side=True, lower=True, transpose_a=True)
        fitted = jnp.dot(stacked_x.astype(jnp.float32), weights.astype(jnp.float32), precision=highest, preferred_element_type=jnp.float32)
        misses = jnp.sum((stacked_y - fitted) ** 2)
        energy = jnp.sum(stacked_y ** 2)
        return (fitted.reshape(2, S, C, H), misses, energy)
    fitted_all, misses_all, energy_all = lax.map(one_pair, (pair_list, ridge_index))
    predicted = jnp.transpose(fitted_all, (2, 3, 4, 1, 0))
    misfit = (jnp.sum(misses_all) / jnp.sum(energy_all)).reshape(1)
    return (predicted, misfit)
```

```python
import math

import jax
import jax.numpy as jnp
import numpy as np
from jax import lax
from jax.experimental import pallas as pl
from jax.experimental.pallas import tpu as pltpu
from jax.sharding import PartitionSpec as P

HIGHEST = lax.Precision.HIGHEST
BLOCK = 32
LANES = 128


def twiddle_rows(length):
    grid = np.arange(length)
    theta = ((grid[:, None] * grid[None, :]) % length) * (2.0 * math.pi / length)
    scaling = 1.0 / math.sqrt(length)
    cosine = np.cos(theta) * scaling
    sine = np.sin(theta) * scaling
    upper = np.concatenate([cosine, -sine], axis=1)
    lower = np.concatenate([sine, cosine], axis=1)
    table = np.concatenate([upper, lower], axis=0)
    return jnp.asarray(np.ascontiguousarray(table.T), dtype=jnp.bfloat16)


def lane_iota(shape):
    return lax.broadcasted_iota(jnp.int32, shape, len(shape) - 1)


def exact_dot(a, b):
    return lax.dot_general(
        a, b, (((1,), (0,)), ((), ())), precision=HIGHEST, preferred_element_type=jnp.float32
    )


def turn(values, amount):
    amount %= LANES
    return pltpu.roll(values, amount, 1) if amount else values


def swap_blocks(values):
    values = list(values)
    lane = lane_iota(values[0].shape)
    for bit in (1, 2, 4):
        odd = (lane & bit) != 0
        for index in range(8):
            if index & bit:
                continue
            low, high = values[index], values[index | bit]
            values[index] = jnp.where(odd, turn(high, bit), low)
            values[index | bit] = jnp.where(odd, high, turn(low, -bit))
    return values


def spectrum_kernel(pairs_ref, table_ref, x_ref, y_ref, out_ref, masked, wide, packed):
    component = pl.program_id(0)

    @pl.when(component == 0)
    def _():
        for j in range(2):
            lanes = pl.ds(j * LANES, LANES)
            mode = pairs_ref[0:1, lanes].astype(jnp.float32)
            wave = pairs_ref[1:2, lanes].astype(jnp.float32)
            mode = jnp.transpose(jnp.broadcast_to(mode, (LANES, LANES)))
            wave = jnp.transpose(jnp.broadcast_to(wave, (LANES, LANES)))
            chosen = wave == lane_iota((LANES, LANES)).astype(jnp.float32)
            chosen = jnp.where(chosen, 1.0, 0.0).astype(jnp.bfloat16)
            mode = jnp.concatenate([mode, mode], axis=1)
            for r in range(2):
                rows = jnp.dot(
                    chosen, table_ref[r * LANES : (r + 1) * LANES, :], preferred_element_type=jnp.float32
                )
                for m in range(16):
                    masked[pl.ds((j * 2 + r) * LANES, LANES), pl.ds(m * 256, 256)] = jnp.where(
                        mode == float(m), rows, 0.0
                    ).astype(jnp.bfloat16)

    for a, ref in enumerate((x_ref, y_ref)):
        wide[...] = ref[...].reshape(4096, LANES).astype(jnp.float32)
        for part in range(32):
            packed[pl.ds(a * LANES, LANES), pl.ds(part * LANES, LANES)] = wide[
                pl.ds(part, LANES, stride=32), :
            ].astype(jnp.bfloat16)
    product = lax.dot_general(
        masked[...], packed[...], (((1,), (1,)), ((), ())), preferred_element_type=jnp.float32
    )
    for a in range(2):
        for q in range(4):
            for group in range(16):
                row = q * LANES + group * 8
                out_ref[pl.ds(group * 8 * 24 + a * 12 + component * 4 + q, 8, stride=24), :] = product[
                    row : row + 8, a * LANES : (a + 1) * LANES
                ]


def invert_block(block):
    shape = block.shape
    lane = lane_iota(shape)
    sub = lax.broadcasted_iota(jnp.int32, shape, 0)
    place = lane & 63
    row_place = place[0:1]
    second = lane >= 64
    for t in range(BLOCK):
        real = jnp.where(second, block[:, 64 + t : 65 + t], block[:, t : t + 1])
        imag = jnp.where(second, block[:, 96 + t : 97 + t], block[:, 32 + t : 33 + t])
        row = block[t : t + 1, :]
        swapped = jnp.where(row_place < 32, -turn(row, -32), turn(row, 32))
        inverse = 1.0 / real[t : t + 1, :]
        at_real = row_place == t
        at_imag = row_place == t + 32
        weight = jnp.where(at_real, inverse, jnp.where(at_imag, 0.0, row * inverse))
        crossed = jnp.where(at_real, 0.0, jnp.where(at_imag, inverse, swapped * inverse))
        cleared = jnp.where((place == t) | (place == t + 32), 0.0, block)
        block = jnp.where(sub == t, weight, cleared - real * weight - imag * crossed)
    return block


def invert(z_ref):
    lane = lane_iota((LANES, LANES))
    sub = lax.broadcasted_iota(jnp.int32, (LANES, LANES), 0)
    for k in range(LANES // BLOCK):
        r = k * BLOCK
        p0, q0 = z_ref[0:128, 0:128], z_ref[0:128, 128:256]
        p1, q1 = z_ref[128:256, 0:128], z_ref[128:256, 128:256]
        zero = jnp.zeros_like(p0)
        first = jnp.where(lane < 32, turn(p0, -r), jnp.where(lane < 64, turn(q0, 32 - r), zero))
        second = jnp.where(lane < 64, zero, jnp.where(lane < 96, turn(p1, 64 - r), turn(q1, 96 - r)))
        diagonal = invert_block(first[r : r + 32] + second[r : r + 32])
        small = lane[0:32]
        left = jnp.concatenate(
            [jnp.where(small < 64, diagonal, 0.0), jnp.where(small < 64, 0.0, diagonal)], axis=0
        )

        def stacked(a, b, c, d):
            return jnp.concatenate(
                [
                    jnp.concatenate([a, b], axis=1),
                    jnp.concatenate([-b, a], axis=1),
                    jnp.concatenate([c, d], axis=1),
                    jnp.concatenate([-d, c], axis=1),
                ],
                axis=0,
            )

        rows = slice(r, r + 32)
        w = exact_dot(left, stacked(p0[rows], q0[rows], p1[rows], q1[rows]))
        here = (small >= r) & (small < r + 32)
        wp0 = jnp.where(here, turn(diagonal, r), w[0:32, 0:128])
        wq0 = jnp.where(here, turn(diagonal, r - 32), w[0:32, 128:256])
        wp1 = jnp.where(here, turn(diagonal, r - 64), w[32:64, 0:128])
        wq1 = jnp.where(here, turn(diagonal, r - 96), w[32:64, 128:256])
        inside = (sub >= r) & (sub < r + 32)
        first = jnp.where(inside, jnp.where(sub - r == lane, -1.0, 0.0), first)
        second = jnp.where(inside, jnp.where(sub - r == lane - 64, -1.0, 0.0), second)
        change = exact_dot(jnp.concatenate([first, second], axis=0), stacked(wp0, wq0, wp1, wq1))
        kept = inside | ((lane >= r) & (lane < r + 32))
        for j in range(2):
            for half in range(2):
                tile = (slice(j * 128, j * 128 + 128), slice(half * 128, half * 128 + 128))
                z_ref[tile] = jnp.where(kept, 0.0, z_ref[tile]) - change[tile]


def solve_kernel(ridge_ref, in_ref, out_ref, fields, gram, z):
    for a in range(2):
        for q in range(4):
            for c in range(3):
                for group in range(2):
                    vectors = swap_blocks(
                        in_ref[pl.ds((snap * 16 + group * 8) * 24 + a * 12 + c * 4 + q, 8, stride=24), :]
                        for snap in range(8)
                    )
                    for h in range(8):
                        fields[a, q, pl.ds(((c * 2 + group) * 8 + h) * 8, 8), :] = vectors[h]

    lane = lane_iota((LANES, LANES))
    sub = lax.broadcasted_iota(jnp.int32, (LANES, LANES), 0)
    diagonal = lane == sub
    large = []
    ridges = []
    for j in range(2):
        at = fields[0, 2 * j]
        bt = fields[0, 2 * j + 1]
        real = jnp.transpose(at)
        imag = jnp.transpose(bt)
        left = jnp.concatenate(
            [jnp.concatenate([real, imag], axis=1), jnp.concatenate([imag, -real], axis=1)], axis=0
        )
        both = exact_dot(left, jnp.concatenate([at, bt], axis=0))
        ridge = ridge_ref[j] * float(LANES)
        ridges.append(ridge)
        rows = slice(j * 128, j * 128 + 128)
        gram[rows, 0:128] = both[0:128]
        gram[rows, 128:256] = both[128:256]
        z[rows, 0:128] = both[0:128] + jnp.where(diagonal, ridge, 0.0)
        z[rows, 128:256] = both[128:256]
        trace = jnp.sum(jnp.where(diagonal, both[0:128], 0.0))
        large.append(trace > ridge * float(LANES))
    invert(z)
    misses = jnp.zeros((8, LANES), jnp.float32)
    energy = jnp.zeros((8, LANES), jnp.float32)
    for j in range(2):
        rows = slice(j * 128, j * 128 + 128)
        p, q = gram[rows, 0:128], gram[rows, 128:256]
        ip, iq = z[rows, 0:128], z[rows, 128:256]
        full = jnp.concatenate(
            [jnp.concatenate([p, q], axis=1), jnp.concatenate([-q, p], axis=1)], axis=0
        )
        direct = exact_dot(jnp.concatenate([ip, iq], axis=1), full)
        tp = jnp.where(large[j], jnp.where(diagonal, 1.0, 0.0) - ridges[j] * ip, direct[:, 0:128])
        tq = jnp.where(large[j], -ridges[j] * iq, direct[:, 128:256])
        target = jnp.concatenate([fields[1, 2 * j], fields[1, 2 * j + 1]], axis=1)
        mixing = jnp.concatenate(
            [jnp.concatenate([tp, tq], axis=1), jnp.concatenate([-tq, tp], axis=1)], axis=0
        )
        fitted = exact_dot(target, mixing)
        missed = (target - fitted) ** 2
        square = target**2
        misses += jnp.sum((missed[:, 0:128] + missed[:, 128:256]).reshape(48, 8, LANES), axis=0)
        energy += jnp.sum((square[:, 0:128] + square[:, 128:256]).reshape(48, 8, LANES), axis=0)
        for r in range(2):
            for c in range(3):
                for group in range(2):
                    vectors = swap_blocks(
                        fitted[((c * 2 + group) * 8 + h) * 8 : ((c * 2 + group) * 8 + h) * 8 + 8, r * 128 : r * 128 + 128]
                        for h in range(8)
                    )
                    for snap in range(8):
                        out_ref[
                            pl.ds((snap * 16 + group * 8) * 13 + c * 4 + 2 * j + r, 8, stride=13), :
                        ] = vectors[snap]
    row = lane[0:8]
    sums = jnp.where(row == 0, jnp.sum(misses), jnp.where(row == 1, jnp.sum(energy), 0.0))
    for group in range(16):
        out_ref[pl.ds(group * 8 * 13 + 12, 8, stride=13), :] = sums


def spread_kernel(in_ref, out_ref, misfit_ref):
    for c in range(3):
        for q in range(4):
            tile = jnp.transpose(in_ref[pl.ds(c * 4 + q, LANES, stride=13), :])
            for s in range(16):
                out_ref[pl.ds(s * 96 + c * 32 + q, 8, stride=4), :] = tile[s * 8 : s * 8 + 8]
    sums = jnp.sum(in_ref[pl.ds(12, LANES, stride=13), :], axis=0, keepdims=True)
    lane = lane_iota((1, LANES))
    misses = jnp.sum(jnp.where(lane == 0, sums, 0.0))
    energy = jnp.sum(jnp.where(lane == 1, sums, 0.0))
    misfit_ref[...] = jnp.full((1, LANES), misses, jnp.float32) / jnp.full((1, LANES), energy, jnp.float32)


def vmem():
    return pl.BlockSpec(memory_space=pltpu.VMEM)


def params(**more):
    return pltpu.CompilerParams(vmem_limit_bytes=56 * 1024 * 1024, **more)


def spectra(pairs, table, resolved, drain):
    block = pl.BlockSpec((16, 1, 256, LANES), lambda c: (0, c, 0, 0))
    whole = lambda shape: pl.BlockSpec(shape, lambda c: (0, 0))
    return pl.pallas_call(
        spectrum_kernel,
        grid=(3,),
        in_specs=[whole((2, 256)), whole((256, 256)), block, block],
        out_specs=whole((3072, LANES)),
        out_shape=jax.ShapeDtypeStruct((3072, LANES), jnp.float32),
        scratch_shapes=[
            pltpu.VMEM((512, 4096), jnp.bfloat16),
            pltpu.VMEM((4096, LANES), jnp.float32),
            pltpu.VMEM((256, 4096), jnp.bfloat16),
        ],
        compiler_params=params(dimension_semantics=("arbitrary",)),
    )(pairs, table, resolved, drain)


def settle(ridge, arrived):
    return pl.pallas_call(
        solve_kernel,
        in_specs=[pl.BlockSpec(memory_space=pltpu.SMEM), vmem()],
        out_specs=vmem(),
        out_shape=jax.ShapeDtypeStruct((1664, LANES), jnp.float32),
        scratch_shapes=[
            pltpu.VMEM((2, 4, 384, LANES), jnp.float32),
            pltpu.VMEM((256, 256), jnp.float32),
            pltpu.VMEM((256, 256), jnp.float32),
        ],
        compiler_params=params(),
    )(ridge, arrived)


def spread(returned):
    return pl.pallas_call(
        spread_kernel,
        in_specs=[vmem()],
        out_specs=(vmem(), vmem()),
        out_shape=(
            jax.ShapeDtypeStruct((1536, LANES), jnp.float32),
            jax.ShapeDtypeStruct((1, LANES), jnp.float32),
        ),
        compiler_params=params(),
    )(returned)


def exchange(values, rows):
    moved = lax.all_to_all(
        values.reshape(128, 1, rows * LANES), ("snap", "height"), split_axis=0, concat_axis=0, tiled=True
    )
    return moved.reshape(128 * rows, LANES)


def per_device(resolved, drain, pair_list, ridge_index):
    table = twiddle_rows(resolved.shape[-1])
    sent = spectra(
        pair_list.T,
        table,
        resolved.reshape(16, 3, 256, LANES),
        drain.reshape(16, 3, 256, LANES),
    )
    owner = lax.axis_index("snap") * 16 + lax.axis_index("height")
    levels = lax.dynamic_slice(ridge_index.reshape(2, 128), (0, owner), (2, 1)).reshape(2)
    ridge = 0.25 * jnp.exp2(levels.astype(jnp.float32))
    fitted = settle(ridge, exchange(sent, 24))
    predicted, misfit = spread(exchange(fitted, 13))
    predicted = predicted.reshape(16, 3, 8, 2, 2, 128).transpose(0, 1, 2, 4, 3, 5)
    return (predicted.reshape(16, 3, 8, 2, 256), misfit[0, 0:1])


def solution(mesh):
    return jax.shard_map(
        per_device,
        mesh=mesh,
        in_specs=(
            P("snap", None, "height", None, None, None),
            P("snap", None, "height", None, None, None),
            P(),
            P(),
        ),
        out_specs=(P("snap", None, "height", None, None), P()),
        check_vma=False,
    )
```

```python
import math

import jax
import jax.numpy as jnp
import numpy as np
from jax import lax
from jax.experimental import pallas as pl
from jax.experimental.pallas import tpu as pltpu
from jax.sharding import PartitionSpec as P

HIGHEST = lax.Precision.HIGHEST
BLOCK = 32
GROUP = 8
LANES = 128
PITCH = 40


def twiddle_rows(length):
    grid = np.arange(length)
    theta = ((grid[:, None] * grid[None, :]) % length) * (2.0 * math.pi / length)
    scaling = 1.0 / math.sqrt(length)
    cosine = np.cos(theta) * scaling
    sine = np.sin(theta) * scaling
    upper = np.concatenate([cosine, -sine], axis=1)
    lower = np.concatenate([sine, cosine], axis=1)
    table = np.concatenate([upper, lower], axis=0)
    return jnp.asarray(np.ascontiguousarray(table.T), dtype=jnp.bfloat16)


def lane_iota(shape):
    return lax.broadcasted_iota(jnp.int32, shape, len(shape) - 1)


def exact_dot(a, b):
    return lax.dot_general(
        a, b, (((1,), (0,)), ((), ())), precision=HIGHEST, preferred_element_type=jnp.float32
    )


def turn(values, amount):
    amount %= LANES
    return pltpu.roll(values, amount, 1) if amount else values


def swap_blocks(values):
    values = list(values)
    lane = lane_iota(values[0].shape)
    for bit in (1, 2, 4):
        odd = (lane & bit) != 0
        for index in range(8):
            if index & bit:
                continue
            low, high = values[index], values[index | bit]
            values[index] = jnp.where(odd, turn(high, bit), low)
            values[index | bit] = jnp.where(odd, high, turn(low, -bit))
    return values


def spectrum_kernel(pairs_ref, table_ref, x_ref, out_ref, masked, wide, packed):
    component = pl.program_id(0)

    @pl.when(component == 0)
    def _():
        for j in range(2):
            lanes = pl.ds(j * LANES, LANES)
            mode = pairs_ref[0:1, lanes].astype(jnp.float32)
            wave = pairs_ref[1:2, lanes].astype(jnp.float32)
            mode = jnp.transpose(jnp.broadcast_to(mode, (LANES, LANES)))
            wave = jnp.transpose(jnp.broadcast_to(wave, (LANES, LANES)))
            chosen = wave == lane_iota((LANES, LANES)).astype(jnp.float32)
            chosen = jnp.where(chosen, 1.0, 0.0).astype(jnp.bfloat16)
            mode = jnp.concatenate([mode, mode], axis=1)
            for r in range(2):
                rows = jnp.dot(
                    chosen, table_ref[r * LANES : (r + 1) * LANES, :], preferred_element_type=jnp.float32
                )
                for m in range(16):
                    masked[pl.ds((j * 2 + r) * LANES, LANES), pl.ds(m * 256, 256)] = jnp.where(
                        mode == float(m), rows, 0.0
                    ).astype(jnp.bfloat16)

    for group in range(128):
        first = group % 8 * 32
        wide[group * PITCH : group * PITCH + 32, :] = x_ref[group // 8, 0, first : first + 32, :].astype(jnp.float32)
    for part in range(32):
        packed[:, pl.ds(part * LANES, LANES)] = wide[pl.ds(part, LANES, stride=PITCH), :].astype(jnp.bfloat16)
    product = lax.dot_general(
        masked[...], packed[...], (((1,), (1,)), ((), ())), preferred_element_type=jnp.float32
    )
    for q in range(4):
        for group in range(16):
            row = q * LANES + group * 8
            out_ref[pl.ds(group * 8 * 12 + component * 4 + q, 8, stride=12), :] = product[row : row + 8, :]


def spread_row(tiles, t):
    return jnp.broadcast_to(tiles[t // 8][t % 8 : t % 8 + 1, :], (8, LANES))


def invert_block(block):
    count = BLOCK // 8
    lane = lane_iota((8, LANES))
    sub = lax.broadcasted_iota(jnp.int32, (8, LANES), 0)
    place = lane & 63
    second = lane >= 64
    tiles = [block[8 * i : 8 * i + 8] for i in range(count)]
    turned = [jnp.where(place < 32, -turn(tile, -32), turn(tile, 32)) for tile in tiles]
    for start in range(0, BLOCK, GROUP):
        columns = []
        for t in range(start, start + GROUP):
            real = [
                jnp.where(
                    second,
                    jnp.broadcast_to(tile[:, 64 + t : 65 + t], (8, LANES)),
                    jnp.broadcast_to(tile[:, t : t + 1], (8, LANES)),
                )
                for tile in tiles
            ]
            imag = [
                jnp.where(
                    second,
                    jnp.broadcast_to(tile[:, 96 + t : 97 + t], (8, LANES)),
                    jnp.broadcast_to(tile[:, 32 + t : 33 + t], (8, LANES)),
                )
                for tile in tiles
            ]
            columns.append((real, imag))
        for step in range(GROUP):
            t = start + step
            real, imag = columns[step]
            pivot = sub == t % 8
            inverse = 1.0 / spread_row(real, t)
            for later in range(step + 1, GROUP):
                other_real, other_imag = columns[later]
                scaled_real = spread_row(other_real, t) * inverse
                scaled_imag = spread_row(other_imag, t) * inverse
                new_real = [o - a * scaled_real + b * scaled_imag for o, a, b in zip(other_real, real, imag)]
                new_imag = [o - a * scaled_imag - b * scaled_real for o, a, b in zip(other_imag, real, imag)]
                new_real[t // 8] = jnp.where(pivot, scaled_real, new_real[t // 8])
                new_imag[t // 8] = jnp.where(pivot, scaled_imag, new_imag[t // 8])
                columns[later] = (new_real, new_imag)
            row = spread_row(tiles, t)
            swapped = spread_row(turned, t)
            at_real = place == t
            at_imag = place == t + 32
            weight = jnp.where(at_real, inverse, jnp.where(at_imag, 0.0, row * inverse))
            crossed = jnp.where(at_real, 0.0, jnp.where(at_imag, inverse, swapped * inverse))
            gone = at_real | at_imag
            tiles = [jnp.where(gone, 0.0, o) - a * weight - b * crossed for o, a, b in zip(tiles, real, imag)]
            tiles[t // 8] = jnp.where(pivot, weight, tiles[t // 8])
            turned = [jnp.where(gone, 0.0, o) - a * crossed + b * weight for o, a, b in zip(turned, real, imag)]
            turned[t // 8] = jnp.where(pivot, crossed, turned[t // 8])
    return jnp.concatenate(tiles, axis=0)


def invert(z_ref):
    lane = lane_iota((LANES, LANES))
    sub = lax.broadcasted_iota(jnp.int32, (LANES, LANES), 0)
    for k in range(LANES // BLOCK):
        r = k * BLOCK
        p0, q0 = z_ref[0:128, 0:128], z_ref[0:128, 128:256]
        p1, q1 = z_ref[128:256, 0:128], z_ref[128:256, 128:256]
        zero = jnp.zeros_like(p0)
        first = jnp.where(lane < 32, turn(p0, -r), jnp.where(lane < 64, turn(q0, 32 - r), zero))
        second = jnp.where(lane < 64, zero, jnp.where(lane < 96, turn(p1, 64 - r), turn(q1, 96 - r)))
        diagonal = invert_block(first[r : r + 32] + second[r : r + 32])
        small = lane[0:32]
        left = jnp.concatenate(
            [jnp.where(small < 64, diagonal, 0.0), jnp.where(small < 64, 0.0, diagonal)], axis=0
        )

        def stacked(a, b, c, d):
            return jnp.concatenate(
                [
                    jnp.concatenate([a, b], axis=1),
                    jnp.concatenate([-b, a], axis=1),
                    jnp.concatenate([c, d], axis=1),
                    jnp.concatenate([-d, c], axis=1),
                ],
                axis=0,
            )

        rows = slice(r, r + 32)
        w = exact_dot(left, stacked(p0[rows], q0[rows], p1[rows], q1[rows]))
        here = (small >= r) & (small < r + 32)
        wp0 = jnp.where(here, turn(diagonal, r), w[0:32, 0:128])
        wq0 = jnp.where(here, turn(diagonal, r - 32), w[0:32, 128:256])
        wp1 = jnp.where(here, turn(diagonal, r - 64), w[32:64, 0:128])
        wq1 = jnp.where(here, turn(diagonal, r - 96), w[32:64, 128:256])
        inside = (sub >= r) & (sub < r + 32)
        first = jnp.where(inside, jnp.where(sub - r == lane, -1.0, 0.0), first)
        second = jnp.where(inside, jnp.where(sub - r == lane - 64, -1.0, 0.0), second)
        change = exact_dot(jnp.concatenate([first, second], axis=0), stacked(wp0, wq0, wp1, wq1))
        kept = inside | ((lane >= r) & (lane < r + 32))
        for j in range(2):
            for half in range(2):
                tile = (slice(j * 128, j * 128 + 128), slice(half * 128, half * 128 + 128))
                z_ref[tile] = jnp.where(kept, 0.0, z_ref[tile]) - change[tile]


def gather_fields(in_ref, fields):
    for q in range(4):
        for c in range(3):
            for group in range(2):
                vectors = swap_blocks(
                    in_ref[pl.ds((snap * 16 + group * 8) * 12 + c * 4 + q, 8, stride=12), :]
                    for snap in range(8)
                )
                for h in range(8):
                    fields[q, pl.ds(((c * 2 + group) * 8 + h) * 8, 8), :] = vectors[h]


def operator_kernel(ridge_ref, in_ref, out_ref, fields, gram, z):
    gather_fields(in_ref, fields)
    lane = lane_iota((LANES, LANES))
    sub = lax.broadcasted_iota(jnp.int32, (LANES, LANES), 0)
    diagonal = lane == sub
    large = []
    ridges = []
    for j in range(2):
        at = fields[2 * j]
        bt = fields[2 * j + 1]
        real = jnp.transpose(at)
        imag = jnp.transpose(bt)
        left = jnp.concatenate(
            [jnp.concatenate([real, imag], axis=1), jnp.concatenate([imag, -real], axis=1)], axis=0
        )
        both = exact_dot(left, jnp.concatenate([at, bt], axis=0))
        ridge = ridge_ref[j] * float(LANES)
        ridges.append(ridge)
        rows = slice(j * 128, j * 128 + 128)
        gram[rows, 0:128] = both[0:128]
        gram[rows, 128:256] = both[128:256]
        z[rows, 0:128] = both[0:128] + jnp.where(diagonal, ridge, 0.0)
        z[rows, 128:256] = both[128:256]
        trace = jnp.sum(jnp.where(diagonal, both[0:128], 0.0))
        large.append(trace > ridge * float(LANES))
    invert(z)
    for j in range(2):
        rows = slice(j * 128, j * 128 + 128)
        p, q = gram[rows, 0:128], gram[rows, 128:256]
        ip, iq = z[rows, 0:128], z[rows, 128:256]
        full = jnp.concatenate(
            [jnp.concatenate([p, q], axis=1), jnp.concatenate([-q, p], axis=1)], axis=0
        )
        direct = exact_dot(jnp.concatenate([ip, iq], axis=1), full)
        out_ref[rows, 0:128] = jnp.where(
            large[j], jnp.where(diagonal, 1.0, 0.0) - ridges[j] * ip, direct[:, 0:128]
        )
        out_ref[rows, 128:256] = jnp.where(large[j], -ridges[j] * iq, direct[:, 128:256])


def fit_kernel(operator_ref, in_ref, out_ref, fields):
    gather_fields(in_ref, fields)
    misses = jnp.zeros((8, LANES), jnp.float32)
    energy = jnp.zeros((8, LANES), jnp.float32)
    for j in range(2):
        rows = slice(j * 128, j * 128 + 128)
        tp, tq = operator_ref[rows, 0:128], operator_ref[rows, 128:256]
        target = jnp.concatenate([fields[2 * j], fields[2 * j + 1]], axis=1)
        mixing = jnp.concatenate(
            [jnp.concatenate([tp, tq], axis=1), jnp.concatenate([-tq, tp], axis=1)], axis=0
        )
        fitted = exact_dot(target, mixing)
        missed = (target - fitted) ** 2
        square = target**2
        misses += jnp.sum((missed[:, 0:128] + missed[:, 128:256]).reshape(48, 8, LANES), axis=0)
        energy += jnp.sum((square[:, 0:128] + square[:, 128:256]).reshape(48, 8, LANES), axis=0)
        for r in range(2):
            for c in range(3):
                for group in range(2):
                    base = (c * 2 + group) * 64
                    vectors = swap_blocks(
                        fitted[base + h * 8 : base + h * 8 + 8, r * 128 : r * 128 + 128] for h in range(8)
                    )
                    for snap in range(8):
                        out_ref[
                            pl.ds((snap * 16 + group * 8) * 13 + c * 4 + 2 * j + r, 8, stride=13), :
                        ] = vectors[snap]
    row = lane_iota((8, LANES))
    sums = jnp.where(row == 0, jnp.sum(misses), jnp.where(row == 1, jnp.sum(energy), 0.0))
    for group in range(16):
        out_ref[pl.ds(group * 8 * 13 + 12, 8, stride=13), :] = sums


def spread_kernel(in_ref, out_ref, misfit_ref):
    for c in range(3):
        for q in range(4):
            tile = jnp.transpose(in_ref[pl.ds(c * 4 + q, LANES, stride=13), :])
            for s in range(16):
                out_ref[pl.ds(s * 96 + c * 32 + q, 8, stride=4), :] = tile[s * 8 : s * 8 + 8]
    sums = jnp.sum(in_ref[pl.ds(12, LANES, stride=13), :], axis=0, keepdims=True)
    lane = lane_iota((1, LANES))
    misses = jnp.sum(jnp.where(lane == 0, sums, 0.0))
    energy = jnp.sum(jnp.where(lane == 1, sums, 0.0))
    misfit_ref[...] = jnp.full((1, LANES), misses, jnp.float32) / jnp.full((1, LANES), energy, jnp.float32)


def vmem():
    return pl.BlockSpec(memory_space=pltpu.VMEM)


def params(**more):
    return pltpu.CompilerParams(vmem_limit_bytes=56 * 1024 * 1024, **more)


def cost(flops, moved):
    return pl.CostEstimate(flops=flops, bytes_accessed=moved, transcendentals=0)


def spectra(pairs, table, field):
    whole = lambda shape: pl.BlockSpec(shape, lambda c: (0, 0))
    return pl.pallas_call(
        spectrum_kernel,
        grid=(3,),
        in_specs=[
            whole((2, 256)),
            whole((256, 256)),
            pl.BlockSpec((16, 1, 256, LANES), lambda c: (0, c, 0, 0)),
        ],
        out_specs=whole((1536, LANES)),
        out_shape=jax.ShapeDtypeStruct((1536, LANES), jnp.float32),
        scratch_shapes=[
            pltpu.VMEM((512, 4096), jnp.bfloat16),
            pltpu.VMEM((128 * PITCH, LANES), jnp.float32),
            pltpu.VMEM((128, 4096), jnp.bfloat16),
        ],
        compiler_params=params(dimension_semantics=("arbitrary",)),
        cost_estimate=cost(5_000_000_000, 30_000_000),
    )(pairs, table, field)


def operators(ridge, arrived):
    return pl.pallas_call(
        operator_kernel,
        in_specs=[pl.BlockSpec(memory_space=pltpu.SMEM), vmem()],
        out_specs=vmem(),
        out_shape=jax.ShapeDtypeStruct((256, 256), jnp.float32),
        scratch_shapes=[
            pltpu.VMEM((4, 384, LANES), jnp.float32),
            pltpu.VMEM((256, 256), jnp.float32),
            pltpu.VMEM((256, 256), jnp.float32),
        ],
        compiler_params=params(),
        cost_estimate=cost(15_000_000_000, 30_000_000),
    )(ridge, arrived)


def fit(operator, arrived):
    return pl.pallas_call(
        fit_kernel,
        in_specs=[vmem(), vmem()],
        out_specs=vmem(),
        out_shape=jax.ShapeDtypeStruct((1664, LANES), jnp.float32),
        scratch_shapes=[pltpu.VMEM((4, 384, LANES), jnp.float32)],
        compiler_params=params(),
    )(operator, arrived)


def spread(returned):
    return pl.pallas_call(
        spread_kernel,
        in_specs=[vmem()],
        out_specs=(vmem(), vmem()),
        out_shape=(
            jax.ShapeDtypeStruct((1536, LANES), jnp.float32),
            jax.ShapeDtypeStruct((1, LANES), jnp.float32),
        ),
        compiler_params=params(),
    )(returned)


def exchange(values, rows):
    moved = lax.all_to_all(
        values.reshape(128, 1, rows * LANES), ("snap", "height"), split_axis=0, concat_axis=0, tiled=True
    )
    return moved.reshape(128 * rows, LANES)


def per_device(resolved, drain, pair_list, ridge_index):
    table = twiddle_rows(resolved.shape[-1])
    pairs = pair_list.T
    sent_x = spectra(pairs, table, resolved.reshape(16, 3, 256, LANES))
    sent_y = spectra(pairs, table, drain.reshape(16, 3, 256, LANES))
    owner = lax.axis_index("snap") * 16 + lax.axis_index("height")
    levels = lax.dynamic_slice(ridge_index.reshape(2, 128), (0, owner), (2, 1)).reshape(2)
    ridge = 0.25 * jnp.exp2(levels.astype(jnp.float32))
    operator = operators(ridge, exchange(sent_x, 12))
    fitted = fit(operator, exchange(sent_y, 12))
    predicted, misfit = spread(exchange(fitted, 13))
    predicted = predicted.reshape(16, 3, 8, 2, 2, 128).transpose(0, 1, 2, 4, 3, 5)
    return (predicted.reshape(16, 3, 8, 2, 256), misfit[0, 0:1])


def solution(mesh):
    return jax.shard_map(
        per_device,
        mesh=mesh,
        in_specs=(
            P("snap", None, "height", None, None, None),
            P("snap", None, "height", None, None, None),
            P(),
            P(),
        ),
        out_specs=(P("snap", None, "height", None, None), P()),
        check_vma=False,
    )
```

```python
import math

import jax
import jax.numpy as jnp
import numpy as np
from jax import lax
from jax.experimental import pallas as pl
from jax.experimental.pallas import tpu as pltpu
from jax.sharding import PartitionSpec as P

HIGHEST = lax.Precision.HIGHEST
BLOCK = 32
LANES = 128
PITCH = 33


def twiddle_rows(length):
    grid = np.arange(length)
    theta = ((grid[:, None] * grid[None, :]) % length) * (2.0 * math.pi / length)
    scaling = 1.0 / math.sqrt(length)
    cosine = np.cos(theta) * scaling
    sine = np.sin(theta) * scaling
    upper = np.concatenate([cosine, -sine], axis=1)
    lower = np.concatenate([sine, cosine], axis=1)
    table = np.concatenate([upper, lower], axis=0)
    return jnp.asarray(np.ascontiguousarray(table.T), dtype=jnp.bfloat16)


def lane_iota(shape):
    return lax.broadcasted_iota(jnp.int32, shape, len(shape) - 1)


def exact_dot(a, b):
    return lax.dot_general(
        a, b, (((1,), (0,)), ((), ())), precision=HIGHEST, preferred_element_type=jnp.float32
    )


def turn(values, amount):
    amount %= LANES
    return pltpu.roll(values, amount, 1) if amount else values


def swap_blocks(values):
    values = list(values)
    lane = lane_iota(values[0].shape)
    for bit in (1, 2, 4):
        odd = (lane & bit) != 0
        for index in range(8):
            if index & bit:
                continue
            low, high = values[index], values[index | bit]
            values[index] = jnp.where(odd, turn(high, bit), low)
            values[index | bit] = jnp.where(odd, high, turn(low, -bit))
    return values


def spectrum_kernel(pairs_ref, table_ref, x_ref, y_ref, out_ref, masked, wide, packed):
    component = pl.program_id(0)

    @pl.when(component == 0)
    def _():
        for j in range(2):
            lanes = pl.ds(j * LANES, LANES)
            mode = pairs_ref[0:1, lanes].astype(jnp.float32)
            wave = pairs_ref[1:2, lanes].astype(jnp.float32)
            mode = jnp.transpose(jnp.broadcast_to(mode, (LANES, LANES)))
            wave = jnp.transpose(jnp.broadcast_to(wave, (LANES, LANES)))
            chosen = wave == lane_iota((LANES, LANES)).astype(jnp.float32)
            chosen = jnp.where(chosen, 1.0, 0.0).astype(jnp.bfloat16)
            mode = jnp.concatenate([mode, mode], axis=1)
            for r in range(2):
                rows = jnp.dot(
                    chosen, table_ref[r * LANES : (r + 1) * LANES, :], preferred_element_type=jnp.float32
                )
                for m in range(16):
                    masked[pl.ds((j * 2 + r) * LANES, LANES), pl.ds(m * 256, 256)] = jnp.where(
                        mode == float(m), rows, 0.0
                    ).astype(jnp.bfloat16)

    for a, ref in enumerate((x_ref, y_ref)):
        for group in range(128):
            first = group % 8 * 32
            wide[group * PITCH : group * PITCH + 32, :] = ref[group // 8, 0, first : first + 32, :].astype(
                jnp.float32
            )
        for part in range(32):
            packed[a * LANES : (a + 1) * LANES, pl.ds(part * LANES, LANES)] = wide[
                pl.ds(part, LANES, stride=PITCH), :
            ].astype(jnp.bfloat16)
    product = lax.dot_general(
        masked[...], packed[...], (((1,), (1,)), ((), ())), preferred_element_type=jnp.float32
    )
    for a in range(2):
        for q in range(4):
            for group in range(16):
                row = q * LANES + group * 8
                out_ref[pl.ds(group * 8 * 24 + a * 12 + component * 4 + q, 8, stride=24), :] = product[
                    row : row + 8, a * LANES : (a + 1) * LANES
                ]


def invert_block(block):
    count = BLOCK // 8
    lane = lane_iota((8, LANES))
    sub = lax.broadcasted_iota(jnp.int32, (8, LANES), 0)
    place = lane & 63
    second = lane >= 64

    def column(tile, t):
        def spread_lane(at):
            return jnp.broadcast_to(tile[:, at : at + 1], (8, LANES))

        return jnp.where(second, spread_lane(64 + t), spread_lane(t))

    def whole_row(tile, t):
        return jnp.broadcast_to(tile[t : t + 1, :], (8, LANES))

    tiles = [block[8 * i : 8 * i + 8] for i in range(count)]
    for g in range(count):
        start = 8 * g
        tile = tiles[g]
        turned = jnp.where(place < 32, -turn(tile, -32), turn(tile, 32))
        columns = [(column(tile, start + t), column(tile, start + t + 32)) for t in range(8)]
        others = {
            i: [(column(tiles[i], start + t), column(tiles[i], start + t + 32)) for t in range(8)]
            for i in range(count)
            if i != g
        }
        for t in range(8):
            real, imag = columns[t]
            pivot = sub == t
            inverse = 1.0 / whole_row(real, t)
            for later in range(t + 1, 8):
                other_real, other_imag = columns[later]
                scaled_real = whole_row(other_real, t) * inverse
                scaled_imag = whole_row(other_imag, t) * inverse
                columns[later] = (
                    jnp.where(pivot, scaled_real, other_real - real * scaled_real + imag * scaled_imag),
                    jnp.where(pivot, scaled_imag, other_imag - real * scaled_imag - imag * scaled_real),
                )
            at_real = place == start + t
            at_imag = place == start + t + 32
            gone = at_real | at_imag
            weight = jnp.where(at_real, inverse, jnp.where(at_imag, 0.0, whole_row(tile, t) * inverse))
            crossed = jnp.where(at_real, 0.0, jnp.where(at_imag, inverse, whole_row(turned, t) * inverse))
            tile = jnp.where(pivot, weight, jnp.where(gone, 0.0, tile) - real * weight - imag * crossed)
            turned = jnp.where(pivot, crossed, jnp.where(gone, 0.0, turned) - real * crossed + imag * weight)
        tiles[g] = tile
        within = place & 31
        gone = (within >= start) & (within < start + 8)
        rows = [(whole_row(tile, t), whole_row(turned, t)) for t in range(8)]
        for i, spreads in others.items():
            changes = [a * weight + b * crossed for (a, b), (weight, crossed) in zip(spreads, rows)]
            while len(changes) > 1:
                changes = [u + v for u, v in zip(changes[::2], changes[1::2])]
            tiles[i] = jnp.where(gone, 0.0, tiles[i]) - changes[0]
    return jnp.concatenate(tiles, axis=0)


def invert(z_ref):
    lane = lane_iota((LANES, LANES))
    sub = lax.broadcasted_iota(jnp.int32, (LANES, LANES), 0)
    for k in range(LANES // BLOCK):
        r = k * BLOCK
        p0, q0 = z_ref[0:128, 0:128], z_ref[0:128, 128:256]
        p1, q1 = z_ref[128:256, 0:128], z_ref[128:256, 128:256]
        zero = jnp.zeros_like(p0)
        first = jnp.where(lane < 32, turn(p0, -r), jnp.where(lane < 64, turn(q0, 32 - r), zero))
        second = jnp.where(lane < 64, zero, jnp.where(lane < 96, turn(p1, 64 - r), turn(q1, 96 - r)))
        diagonal = invert_block(first[r : r + 32] + second[r : r + 32])
        small = lane[0:32]
        left = jnp.concatenate(
            [jnp.where(small < 64, diagonal, 0.0), jnp.where(small < 64, 0.0, diagonal)], axis=0
        )

        def stacked(a, b, c, d):
            return jnp.concatenate(
                [
                    jnp.concatenate([a, b], axis=1),
                    jnp.concatenate([-b, a], axis=1),
                    jnp.concatenate([c, d], axis=1),
                    jnp.concatenate([-d, c], axis=1),
                ],
                axis=0,
            )

        rows = slice(r, r + 32)
        w = exact_dot(left, stacked(p0[rows], q0[rows], p1[rows], q1[rows]))
        here = (small >= r) & (small < r + 32)
        wp0 = jnp.where(here, turn(diagonal, r), w[0:32, 0:128])
        wq0 = jnp.where(here, turn(diagonal, r - 32), w[0:32, 128:256])
        wp1 = jnp.where(here, turn(diagonal, r - 64), w[32:64, 0:128])
        wq1 = jnp.where(here, turn(diagonal, r - 96), w[32:64, 128:256])
        inside = (sub >= r) & (sub < r + 32)
        first = jnp.where(inside, jnp.where(sub - r == lane, -1.0, 0.0), first)
        second = jnp.where(inside, jnp.where(sub - r == lane - 64, -1.0, 0.0), second)
        change = exact_dot(jnp.concatenate([first, second], axis=0), stacked(wp0, wq0, wp1, wq1))
        kept = inside | ((lane >= r) & (lane < r + 32))
        for j in range(2):
            for half in range(2):
                tile = (slice(j * 128, j * 128 + 128), slice(half * 128, half * 128 + 128))
                z_ref[tile] = jnp.where(kept, 0.0, z_ref[tile]) - change[tile]


def gather_fields(in_ref, fields, a):
    for q in range(4):
        for c in range(3):
            for group in range(2):
                vectors = swap_blocks(
                    in_ref[pl.ds((snap * 16 + group * 8) * 24 + a * 12 + c * 4 + q, 8, stride=24), :]
                    for snap in range(8)
                )
                for h in range(8):
                    fields[a, q, pl.ds(((c * 2 + group) * 8 + h) * 8, 8), :] = vectors[h]


def solve_kernel(ridge_ref, in_ref, out_ref, fields, gram, z):
    gather_fields(in_ref, fields, 0)
    owner = lax.axis_index("snap") * 16 + lax.axis_index("height")
    lane = lane_iota((LANES, LANES))
    sub = lax.broadcasted_iota(jnp.int32, (LANES, LANES), 0)
    diagonal = lane == sub
    large = []
    ridges = []
    for j in range(2):
        at = fields[0, 2 * j]
        bt = fields[0, 2 * j + 1]
        real = jnp.transpose(at)
        imag = jnp.transpose(bt)
        left = jnp.concatenate(
            [jnp.concatenate([real, imag], axis=1), jnp.concatenate([imag, -real], axis=1)], axis=0
        )
        both = exact_dot(left, jnp.concatenate([at, bt], axis=0))
        ridge = lax.shift_left(jnp.int32(LANES // 4), ridge_ref[j * LANES + owner]).astype(jnp.float32)
        ridges.append(ridge)
        rows = slice(j * 128, j * 128 + 128)
        gram[rows, 0:128] = both[0:128]
        gram[rows, 128:256] = both[128:256]
        z[rows, 0:128] = both[0:128] + jnp.where(diagonal, ridge, 0.0)
        z[rows, 128:256] = both[128:256]
        trace = jnp.sum(jnp.where(diagonal, both[0:128], 0.0))
        large.append(trace > ridge * float(LANES))
    gather_fields(in_ref, fields, 1)
    invert(z)
    misses = jnp.zeros((8, LANES), jnp.float32)
    energy = jnp.zeros((8, LANES), jnp.float32)
    for j in range(2):
        rows = slice(j * 128, j * 128 + 128)
        p, q = gram[rows, 0:128], gram[rows, 128:256]
        ip, iq = z[rows, 0:128], z[rows, 128:256]
        full = jnp.concatenate(
            [jnp.concatenate([p, q], axis=1), jnp.concatenate([-q, p], axis=1)], axis=0
        )
        direct = exact_dot(jnp.concatenate([ip, iq], axis=1), full)
        tp = jnp.where(large[j], jnp.where(diagonal, 1.0, 0.0) - ridges[j] * ip, direct[:, 0:128])
        tq = jnp.where(large[j], -ridges[j] * iq, direct[:, 128:256])
        target = jnp.concatenate([fields[1, 2 * j], fields[1, 2 * j + 1]], axis=1)
        mixing = jnp.concatenate(
            [jnp.concatenate([tp, tq], axis=1), jnp.concatenate([-tq, tp], axis=1)], axis=0
        )
        fitted = exact_dot(target, mixing)
        missed = (target - fitted) ** 2
        square = target**2
        misses += jnp.sum((missed[:, 0:128] + missed[:, 128:256]).reshape(48, 8, LANES), axis=0)
        energy += jnp.sum((square[:, 0:128] + square[:, 128:256]).reshape(48, 8, LANES), axis=0)
        for r in range(2):
            for c in range(3):
                for group in range(2):
                    base = (c * 2 + group) * 64
                    vectors = swap_blocks(
                        fitted[base + h * 8 : base + h * 8 + 8, r * 128 : r * 128 + 128] for h in range(8)
                    )
                    for snap in range(8):
                        out_ref[
                            pl.ds((snap * 16 + group * 8) * 13 + c * 4 + 2 * j + r, 8, stride=13), :
                        ] = vectors[snap]
    row = lane_iota((8, LANES))
    sums = jnp.where(row == 0, jnp.sum(misses), jnp.where(row == 1, jnp.sum(energy), 0.0))
    for group in range(16):
        out_ref[pl.ds(group * 8 * 13 + 12, 8, stride=13), :] = sums


def spread_kernel(in_ref, out_ref, misfit_ref):
    for c in range(3):
        for q in range(4):
            tile = jnp.transpose(in_ref[pl.ds(c * 4 + q, LANES, stride=13), :])
            for s in range(16):
                out_ref[pl.ds(s * 96 + c * 32 + q, 8, stride=4), :] = tile[s * 8 : s * 8 + 8]
    sums = jnp.sum(in_ref[pl.ds(12, LANES, stride=13), :], axis=0, keepdims=True)
    lane = lane_iota((1, LANES))
    misses = jnp.sum(jnp.where(lane == 0, sums, 0.0))
    energy = jnp.sum(jnp.where(lane == 1, sums, 0.0))
    misfit_ref[...] = jnp.full((1, LANES), misses, jnp.float32) / jnp.full((1, LANES), energy, jnp.float32)


def vmem():
    return pl.BlockSpec(memory_space=pltpu.VMEM)


def params(megabytes, **more):
    return pltpu.CompilerParams(vmem_limit_bytes=megabytes * 1024 * 1024, **more)


def spectra(pairs, table, resolved, drain):
    block = pl.BlockSpec((16, 1, 256, LANES), lambda c: (0, c, 0, 0))
    whole = lambda shape: pl.BlockSpec(shape, lambda c: (0, 0))
    return pl.pallas_call(
        spectrum_kernel,
        grid=(3,),
        in_specs=[whole((2, 256)), whole((256, 256)), block, block],
        out_specs=whole((3072, LANES)),
        out_shape=jax.ShapeDtypeStruct((3072, LANES), jnp.float32),
        scratch_shapes=[
            pltpu.VMEM((512, 4096), jnp.bfloat16),
            pltpu.VMEM((128 * PITCH, LANES), jnp.float32),
            pltpu.VMEM((256, 4096), jnp.bfloat16),
        ],
        compiler_params=params(56, dimension_semantics=("arbitrary",)),
    )(pairs, table, resolved, drain)


def settle(ridge_index, arrived):
    return pl.pallas_call(
        solve_kernel,
        in_specs=[pl.BlockSpec(memory_space=pltpu.SMEM), vmem()],
        out_specs=vmem(),
        out_shape=jax.ShapeDtypeStruct((1664, LANES), jnp.float32),
        scratch_shapes=[
            pltpu.VMEM((2, 4, 384, LANES), jnp.float32),
            pltpu.VMEM((256, 256), jnp.float32),
            pltpu.VMEM((256, 256), jnp.float32),
        ],
        compiler_params=params(24),
    )(ridge_index, arrived)


def spread(returned):
    return pl.pallas_call(
        spread_kernel,
        in_specs=[vmem()],
        out_specs=(vmem(), vmem()),
        out_shape=(
            jax.ShapeDtypeStruct((1536, LANES), jnp.float32),
            jax.ShapeDtypeStruct((1, LANES), jnp.float32),
        ),
        compiler_params=params(24),
    )(returned)


def exchange(values, rows):
    moved = lax.all_to_all(
        values.reshape(128, 1, rows * LANES), ("snap", "height"), split_axis=0, concat_axis=0, tiled=True
    )
    return moved.reshape(128 * rows, LANES)


def per_device(resolved, drain, pair_list, ridge_index):
    table = twiddle_rows(resolved.shape[-1])
    pairs = pair_list.T
    sent = spectra(
        pairs, table, resolved.reshape(16, 3, 256, LANES), drain.reshape(16, 3, 256, LANES)
    )
    fitted = settle(ridge_index, exchange(sent, 24))
    predicted, misfit = spread(exchange(fitted, 13))
    predicted = predicted.reshape(16, 3, 8, 2, 2, 128).transpose(0, 1, 2, 4, 3, 5)
    return (predicted.reshape(16, 3, 8, 2, 256), misfit[0, 0:1])


def solution(mesh):
    return jax.shard_map(
        per_device,
        mesh=mesh,
        in_specs=(
            P("snap", None, "height", None, None, None),
            P("snap", None, "height", None, None, None),
            P(),
            P(),
        ),
        out_specs=(P("snap", None, "height", None, None), P()),
        check_vma=False,
    )
```

```python
import math

import jax
import jax.numpy as jnp
import numpy as np
from jax import lax
from jax.experimental import pallas as pl
from jax.experimental.pallas import tpu as pltpu
from jax.sharding import PartitionSpec as P

HIGHEST = lax.Precision.HIGHEST
BLOCK = 32
LANES = 128
PITCH = 33


def twiddle_rows(length):
    grid = np.arange(length)
    theta = ((grid[:, None] * grid[None, :]) % length) * (2.0 * math.pi / length)
    scaling = 1.0 / math.sqrt(length)
    cosine = np.cos(theta) * scaling
    sine = np.sin(theta) * scaling
    upper = np.concatenate([cosine, -sine], axis=1)
    lower = np.concatenate([sine, cosine], axis=1)
    table = np.concatenate([upper, lower], axis=0)
    return jnp.asarray(np.ascontiguousarray(table.T), dtype=jnp.bfloat16)


def lane_iota(shape):
    return lax.broadcasted_iota(jnp.int32, shape, len(shape) - 1)


def exact_dot(a, b):
    return lax.dot_general(
        a, b, (((1,), (0,)), ((), ())), precision=HIGHEST, preferred_element_type=jnp.float32
    )


def turn(values, amount):
    amount %= LANES
    return pltpu.roll(values, amount, 1) if amount else values


def swap_blocks(values):
    values = list(values)
    lane = lane_iota(values[0].shape)
    for bit in (1, 2, 4):
        odd = (lane & bit) != 0
        for index in range(8):
            if index & bit:
                continue
            low, high = values[index], values[index | bit]
            values[index] = jnp.where(odd, turn(high, bit), low)
            values[index | bit] = jnp.where(odd, high, turn(low, -bit))
    return values


def spectrum_kernel(pairs_ref, table_ref, x_ref, y_ref, out_ref, masked, wide, packed):
    component = pl.program_id(0)

    @pl.when(component == 0)
    def _():
        for j in range(2):
            lanes = pl.ds(j * LANES, LANES)
            mode = pairs_ref[0:1, lanes].astype(jnp.float32)
            wave = pairs_ref[1:2, lanes].astype(jnp.float32)
            mode = jnp.transpose(jnp.broadcast_to(mode, (LANES, LANES)))
            wave = jnp.transpose(jnp.broadcast_to(wave, (LANES, LANES)))
            chosen = wave == lane_iota((LANES, LANES)).astype(jnp.float32)
            chosen = jnp.where(chosen, 1.0, 0.0).astype(jnp.bfloat16)
            mode = jnp.concatenate([mode, mode], axis=1)
            for r in range(2):
                rows = jnp.dot(
                    chosen, table_ref[r * LANES : (r + 1) * LANES, :], preferred_element_type=jnp.float32
                )
                for m in range(16):
                    masked[pl.ds((j * 2 + r) * LANES, LANES), pl.ds(m * 256, 256)] = jnp.where(
                        mode == float(m), rows, 0.0
                    ).astype(jnp.bfloat16)

    for a, ref in enumerate((x_ref, y_ref)):
        for group in range(128):
            first = group % 8 * 32
            wide[group * PITCH : group * PITCH + 32, :] = ref[group // 8, 0, first : first + 32, :].astype(
                jnp.float32
            )
        for part in range(32):
            packed[a * LANES : (a + 1) * LANES, pl.ds(part * LANES, LANES)] = wide[
                pl.ds(part, LANES, stride=PITCH), :
            ].astype(jnp.bfloat16)
    product = lax.dot_general(
        masked[...], packed[...], (((1,), (1,)), ((), ())), preferred_element_type=jnp.float32
    )
    for a in range(2):
        for q in range(4):
            for group in range(16):
                row = q * LANES + group * 8
                out_ref[pl.ds(group * 8 * 24 + a * 12 + component * 4 + q, 8, stride=24), :] = product[
                    row : row + 8, a * LANES : (a + 1) * LANES
                ]


def invert_block(block):
    count = BLOCK // 8
    lane = lane_iota((8, LANES))
    sub = lax.broadcasted_iota(jnp.int32, (8, LANES), 0)
    place = lane & 63
    second = lane >= 64

    def column(tile, t):
        def spread_lane(at):
            return jnp.broadcast_to(tile[:, at : at + 1], (8, LANES))

        return jnp.where(second, spread_lane(64 + t), spread_lane(t))

    def whole_row(tile, t):
        return jnp.broadcast_to(tile[t : t + 1, :], (8, LANES))

    tiles = [block[8 * i : 8 * i + 8] for i in range(count)]
    for g in range(count):
        start = 8 * g
        tile = tiles[g]
        turned = jnp.where(place < 32, -turn(tile, -32), turn(tile, 32))
        columns = [(column(tile, start + t), column(tile, start + t + 32)) for t in range(8)]
        others = {
            i: [(column(tiles[i], start + t), column(tiles[i], start + t + 32)) for t in range(8)]
            for i in range(count)
            if i != g
        }
        for t in range(8):
            real, imag = columns[t]
            pivot = sub == t
            inverse = 1.0 / whole_row(real, t)
            for later in range(t + 1, 8):
                other_real, other_imag = columns[later]
                scaled_real = whole_row(other_real, t) * inverse
                scaled_imag = whole_row(other_imag, t) * inverse
                columns[later] = (
                    jnp.where(pivot, scaled_real, other_real - real * scaled_real + imag * scaled_imag),
                    jnp.where(pivot, scaled_imag, other_imag - real * scaled_imag - imag * scaled_real),
                )
            at_real = place == start + t
            at_imag = place == start + t + 32
            gone = at_real | at_imag
            weight = jnp.where(at_real, inverse, jnp.where(at_imag, 0.0, whole_row(tile, t) * inverse))
            crossed = jnp.where(at_real, 0.0, jnp.where(at_imag, inverse, whole_row(turned, t) * inverse))
            tile = jnp.where(pivot, weight, jnp.where(gone, 0.0, tile) - real * weight - imag * crossed)
            turned = jnp.where(pivot, crossed, jnp.where(gone, 0.0, turned) - real * crossed + imag * weight)
        tiles[g] = tile
        within = place & 31
        gone = (within >= start) & (within < start + 8)
        rows = [(whole_row(tile, t), whole_row(turned, t)) for t in range(8)]
        for i, spreads in others.items():
            changes = [a * weight + b * crossed for (a, b), (weight, crossed) in zip(spreads, rows)]
            while len(changes) > 1:
                changes = [u + v for u, v in zip(changes[::2], changes[1::2])]
            tiles[i] = jnp.where(gone, 0.0, tiles[i]) - changes[0]
    return jnp.concatenate(tiles, axis=0)


def invert(z_ref):
    lane = lane_iota((LANES, LANES))
    sub = lax.broadcasted_iota(jnp.int32, (LANES, LANES), 0)
    for k in range(LANES // BLOCK):
        r = k * BLOCK
        p0, q0 = z_ref[0:128, 0:128], z_ref[0:128, 128:256]
        p1, q1 = z_ref[128:256, 0:128], z_ref[128:256, 128:256]
        zero = jnp.zeros_like(p0)
        first = jnp.where(lane < 32, turn(p0, -r), jnp.where(lane < 64, turn(q0, 32 - r), zero))
        second = jnp.where(lane < 64, zero, jnp.where(lane < 96, turn(p1, 64 - r), turn(q1, 96 - r)))
        diagonal = invert_block(first[r : r + 32] + second[r : r + 32])
        small = lane[0:32]
        left = jnp.concatenate(
            [jnp.where(small < 64, diagonal, 0.0), jnp.where(small < 64, 0.0, diagonal)], axis=0
        )

        def stacked(a, b, c, d):
            return jnp.concatenate(
                [
                    jnp.concatenate([a, b], axis=1),
                    jnp.concatenate([-b, a], axis=1),
                    jnp.concatenate([c, d], axis=1),
                    jnp.concatenate([-d, c], axis=1),
                ],
                axis=0,
            )

        rows = slice(r, r + 32)
        w = exact_dot(left, stacked(p0[rows], q0[rows], p1[rows], q1[rows]))
        here = (small >= r) & (small < r + 32)
        wp0 = jnp.where(here, turn(diagonal, r), w[0:32, 0:128])
        wq0 = jnp.where(here, turn(diagonal, r - 32), w[0:32, 128:256])
        wp1 = jnp.where(here, turn(diagonal, r - 64), w[32:64, 0:128])
        wq1 = jnp.where(here, turn(diagonal, r - 96), w[32:64, 128:256])
        inside = (sub >= r) & (sub < r + 32)
        first = jnp.where(inside, jnp.where(sub - r == lane, -1.0, 0.0), first)
        second = jnp.where(inside, jnp.where(sub - r == lane - 64, -1.0, 0.0), second)
        change = exact_dot(jnp.concatenate([first, second], axis=0), stacked(wp0, wq0, wp1, wq1))
        kept = inside | ((lane >= r) & (lane < r + 32))
        for j in range(2):
            for half in range(2):
                tile = (slice(j * 128, j * 128 + 128), slice(half * 128, half * 128 + 128))
                z_ref[tile] = jnp.where(kept, 0.0, z_ref[tile]) - change[tile]


def gather_fields(in_ref, fields, a):
    for q in range(4):
        for c in range(3):
            for group in range(2):
                vectors = swap_blocks(
                    in_ref[pl.ds((snap * 16 + group * 8) * 24 + a * 12 + c * 4 + q, 8, stride=24), :]
                    for snap in range(8)
                )
                for h in range(8):
                    fields[a, q, pl.ds(((c * 2 + group) * 8 + h) * 8, 8), :] = vectors[h]


def solve_kernel(ridge_ref, in_ref, out_ref, fields, gram, z):
    gather_fields(in_ref, fields, 0)
    owner = lax.axis_index("snap") * 16 + lax.axis_index("height")
    lane = lane_iota((LANES, LANES))
    sub = lax.broadcasted_iota(jnp.int32, (LANES, LANES), 0)
    diagonal = lane == sub
    large = []
    ridges = []
    for j in range(2):
        at = fields[0, 2 * j]
        bt = fields[0, 2 * j + 1]
        real = jnp.transpose(at)
        imag = jnp.transpose(bt)
        product = exact_dot(jnp.concatenate([real, imag], axis=0), jnp.concatenate([at, bt], axis=1))
        p = product[0:128, 0:128] + product[128:256, 128:256]
        q = product[128:256, 0:128] - product[0:128, 128:256]
        ridge = lax.shift_left(jnp.int32(LANES // 4), ridge_ref[j * LANES + owner]).astype(jnp.float32)
        ridges.append(ridge)
        rows = slice(j * 128, j * 128 + 128)
        gram[rows, 0:128] = p
        gram[rows, 128:256] = q
        z[rows, 0:128] = p + jnp.where(diagonal, ridge, 0.0)
        z[rows, 128:256] = q
        trace = jnp.sum(jnp.where(diagonal, p, 0.0))
        large.append(trace > ridge * float(LANES))
    gather_fields(in_ref, fields, 1)
    invert(z)
    misses = jnp.zeros((8, LANES), jnp.float32)
    energy = jnp.zeros((8, LANES), jnp.float32)
    for j in range(2):
        rows = slice(j * 128, j * 128 + 128)
        ridge = ridges[j]

        @pl.when(large[j])
        def _():
            z[rows, 0:128] = jnp.where(diagonal, 1.0, 0.0) - ridge * z[rows, 0:128]
            z[rows, 128:256] = -ridge * z[rows, 128:256]

        @pl.when(jnp.logical_not(large[j]))
        def _():
            p, q = gram[rows, 0:128], gram[rows, 128:256]
            full = jnp.concatenate(
                [jnp.concatenate([p, q], axis=1), jnp.concatenate([-q, p], axis=1)], axis=0
            )
            z[rows, :] = exact_dot(z[rows, :], full)

        tp, tq = z[rows, 0:128], z[rows, 128:256]
        target = jnp.concatenate([fields[1, 2 * j], fields[1, 2 * j + 1]], axis=1)
        mixing = jnp.concatenate(
            [jnp.concatenate([tp, tq], axis=1), jnp.concatenate([-tq, tp], axis=1)], axis=0
        )
        fitted = exact_dot(target, mixing)
        missed = (target - fitted) ** 2
        square = target**2
        misses += jnp.sum((missed[:, 0:128] + missed[:, 128:256]).reshape(48, 8, LANES), axis=0)
        energy += jnp.sum((square[:, 0:128] + square[:, 128:256]).reshape(48, 8, LANES), axis=0)
        for r in range(2):
            for c in range(3):
                for group in range(2):
                    base = (c * 2 + group) * 64
                    vectors = swap_blocks(
                        fitted[base + h * 8 : base + h * 8 + 8, r * 128 : r * 128 + 128] for h in range(8)
                    )
                    for snap in range(8):
                        out_ref[
                            pl.ds((snap * 16 + group * 8) * 13 + c * 4 + 2 * j + r, 8, stride=13), :
                        ] = vectors[snap]
    row = lane_iota((8, LANES))
    sums = jnp.where(row == 0, jnp.sum(misses), jnp.where(row == 1, jnp.sum(energy), 0.0))
    for group in range(16):
        out_ref[pl.ds(group * 8 * 13 + 12, 8, stride=13), :] = sums


def spread_kernel(in_ref, out_ref, misfit_ref):
    for c in range(3):
        for q in range(4):
            tile = jnp.transpose(in_ref[pl.ds(c * 4 + q, LANES, stride=13), :])
            for s in range(16):
                out_ref[pl.ds(s * 96 + c * 32 + q, 8, stride=4), :] = tile[s * 8 : s * 8 + 8]
    sums = jnp.sum(in_ref[pl.ds(12, LANES, stride=13), :], axis=0, keepdims=True)
    lane = lane_iota((1, LANES))
    misses = jnp.sum(jnp.where(lane == 0, sums, 0.0))
    energy = jnp.sum(jnp.where(lane == 1, sums, 0.0))
    misfit_ref[...] = jnp.full((1, LANES), misses, jnp.float32) / jnp.full((1, LANES), energy, jnp.float32)


def vmem():
    return pl.BlockSpec(memory_space=pltpu.VMEM)


def params(megabytes, **more):
    return pltpu.CompilerParams(vmem_limit_bytes=megabytes * 1024 * 1024, **more)


def spectra(pairs, table, resolved, drain):
    block = pl.BlockSpec((16, 1, 256, LANES), lambda c: (0, c, 0, 0))
    whole = lambda shape: pl.BlockSpec(shape, lambda c: (0, 0))
    return pl.pallas_call(
        spectrum_kernel,
        grid=(3,),
        in_specs=[whole((2, 256)), whole((256, 256)), block, block],
        out_specs=whole((3072, LANES)),
        out_shape=jax.ShapeDtypeStruct((3072, LANES), jnp.float32),
        scratch_shapes=[
            pltpu.VMEM((512, 4096), jnp.bfloat16),
            pltpu.VMEM((128 * PITCH, LANES), jnp.float32),
            pltpu.VMEM((256, 4096), jnp.bfloat16),
        ],
        compiler_params=params(56, dimension_semantics=("arbitrary",)),
    )(pairs, table, resolved, drain)


def settle(ridge_index, arrived):
    return pl.pallas_call(
        solve_kernel,
        in_specs=[pl.BlockSpec(memory_space=pltpu.SMEM), vmem()],
        out_specs=vmem(),
        out_shape=jax.ShapeDtypeStruct((1664, LANES), jnp.float32),
        scratch_shapes=[
            pltpu.VMEM((2, 4, 384, LANES), jnp.float32),
            pltpu.VMEM((256, 256), jnp.float32),
            pltpu.VMEM((256, 256), jnp.float32),
        ],
        compiler_params=params(24),
    )(ridge_index, arrived)


def spread(returned):
    return pl.pallas_call(
        spread_kernel,
        in_specs=[vmem()],
        out_specs=(vmem(), vmem()),
        out_shape=(
            jax.ShapeDtypeStruct((1536, LANES), jnp.float32),
            jax.ShapeDtypeStruct((1, LANES), jnp.float32),
        ),
        compiler_params=params(24),
    )(returned)


def exchange(values, rows):
    moved = lax.all_to_all(
        values.reshape(128, 1, rows * LANES), ("snap", "height"), split_axis=0, concat_axis=0, tiled=True
    )
    return moved.reshape(128 * rows, LANES)


def per_device(resolved, drain, pair_list, ridge_index):
    table = twiddle_rows(resolved.shape[-1])
    pairs = pair_list.T
    sent = spectra(
        pairs, table, resolved.reshape(16, 3, 256, LANES), drain.reshape(16, 3, 256, LANES)
    )
    fitted = settle(ridge_index, exchange(sent, 24))
    predicted, misfit = spread(exchange(fitted, 13))
    predicted = predicted.reshape(16, 3, 8, 2, 2, 128).transpose(0, 1, 2, 4, 3, 5)
    return (predicted.reshape(16, 3, 8, 2, 256), misfit[0, 0:1])


def solution(mesh):
    return jax.shard_map(
        per_device,
        mesh=mesh,
        in_specs=(
            P("snap", None, "height", None, None, None),
            P("snap", None, "height", None, None, None),
            P(),
            P(),
        ),
        out_specs=(P("snap", None, "height", None, None), P()),
        check_vma=False,
    )
```

```python
import math

import jax
import jax.numpy as jnp
import numpy as np
from jax import lax
from jax.experimental import pallas as pl
from jax.experimental.pallas import tpu as pltpu
from jax.sharding import PartitionSpec as P

HIGHEST = lax.Precision.HIGHEST
BLOCK = 32
LANES = 128
PITCH = 33


def twiddle_rows(length):
    grid = np.arange(length)
    theta = ((grid[:, None] * grid[None, :]) % length) * (2.0 * math.pi / length)
    scaling = 1.0 / math.sqrt(length)
    cosine = np.cos(theta) * scaling
    sine = np.sin(theta) * scaling
    upper = np.concatenate([cosine, -sine], axis=1)
    lower = np.concatenate([sine, cosine], axis=1)
    table = np.concatenate([upper, lower], axis=0)
    return jnp.asarray(np.ascontiguousarray(table.T), dtype=jnp.bfloat16)


def lane_iota(shape):
    return lax.broadcasted_iota(jnp.int32, shape, len(shape) - 1)


def exact_dot(a, b):
    return lax.dot_general(
        a, b, (((1,), (0,)), ((), ())), precision=HIGHEST, preferred_element_type=jnp.float32
    )


def turn(values, amount):
    amount %= LANES
    return pltpu.roll(values, amount, 1) if amount else values


def swap_blocks(values):
    values = list(values)
    lane = lane_iota(values[0].shape)
    for bit in (1, 2, 4):
        odd = (lane & bit) != 0
        for index in range(8):
            if index & bit:
                continue
            low, high = values[index], values[index | bit]
            values[index] = jnp.where(odd, turn(high, bit), low)
            values[index | bit] = jnp.where(odd, high, turn(low, -bit))
    return values


def spectrum_kernel(pairs_ref, table_ref, x_ref, y_ref, out_ref, masked, wide, packed):
    component = pl.program_id(0)

    @pl.when(component == 0)
    def _():
        for j in range(2):
            lanes = pl.ds(j * LANES, LANES)
            mode = pairs_ref[0:1, lanes].astype(jnp.float32)
            wave = pairs_ref[1:2, lanes].astype(jnp.float32)
            mode = jnp.transpose(jnp.broadcast_to(mode, (LANES, LANES)))
            wave = jnp.transpose(jnp.broadcast_to(wave, (LANES, LANES)))
            chosen = wave == lane_iota((LANES, LANES)).astype(jnp.float32)
            chosen = jnp.where(chosen, 1.0, 0.0).astype(jnp.bfloat16)
            mode = jnp.concatenate([mode, mode], axis=1)
            for r in range(2):
                rows = jnp.dot(
                    chosen, table_ref[r * LANES : (r + 1) * LANES, :], preferred_element_type=jnp.float32
                )
                for m in range(16):
                    masked[pl.ds((j * 2 + r) * LANES, LANES), pl.ds(m * 256, 256)] = jnp.where(
                        mode == float(m), rows, 0.0
                    ).astype(jnp.bfloat16)

    for a, ref in enumerate((x_ref, y_ref)):
        for group in range(128):
            first = group % 8 * 32
            wide[group * PITCH : group * PITCH + 32, :] = ref[group // 8, 0, first : first + 32, :].astype(
                jnp.float32
            )
        for part in range(32):
            packed[a * LANES : (a + 1) * LANES, pl.ds(part * LANES, LANES)] = wide[
                pl.ds(part, LANES, stride=PITCH), :
            ].astype(jnp.bfloat16)
    product = lax.dot_general(
        masked[...], packed[...], (((1,), (1,)), ((), ())), preferred_element_type=jnp.float32
    )
    for a in range(2):
        for q in range(4):
            for group in range(16):
                row = q * LANES + group * 8
                out_ref[pl.ds(group * 8 * 24 + a * 12 + component * 4 + q, 8, stride=24), :] = product[
                    row : row + 8, a * LANES : (a + 1) * LANES
                ]


def invert_block(block):
    count = BLOCK // 8
    lane = lane_iota((8, LANES))
    sub = lax.broadcasted_iota(jnp.int32, (8, LANES), 0)
    place = lane & 63
    second = lane >= 64

    def column(tile, t):
        def spread_lane(at):
            return jnp.broadcast_to(tile[:, at : at + 1], (8, LANES))

        return jnp.where(second, spread_lane(64 + t), spread_lane(t))

    def whole_row(tile, t):
        return jnp.broadcast_to(tile[t : t + 1, :], (8, LANES))

    tiles = [block[8 * i : 8 * i + 8] for i in range(count)]
    for g in range(count):
        start = 8 * g
        tile = tiles[g]
        turned = jnp.where(place < 32, -turn(tile, -32), turn(tile, 32))
        columns = [(column(tile, start + t), column(tile, start + t + 32)) for t in range(8)]
        others = {
            i: [(column(tiles[i], start + t), column(tiles[i], start + t + 32)) for t in range(8)]
            for i in range(count)
            if i != g
        }
        for t in range(8):
            real, imag = columns[t]
            pivot = sub == t
            inverse = 1.0 / whole_row(real, t)
            for later in range(t + 1, 8):
                other_real, other_imag = columns[later]
                scaled_real = whole_row(other_real, t) * inverse
                scaled_imag = whole_row(other_imag, t) * inverse
                columns[later] = (
                    jnp.where(pivot, scaled_real, other_real - real * scaled_real + imag * scaled_imag),
                    jnp.where(pivot, scaled_imag, other_imag - real * scaled_imag - imag * scaled_real),
                )
            at_real = place == start + t
            at_imag = place == start + t + 32
            gone = at_real | at_imag
            weight = jnp.where(at_real, inverse, jnp.where(at_imag, 0.0, whole_row(tile, t) * inverse))
            crossed = jnp.where(at_real, 0.0, jnp.where(at_imag, inverse, whole_row(turned, t) * inverse))
            tile = jnp.where(pivot, weight, jnp.where(gone, 0.0, tile) - real * weight - imag * crossed)
            turned = jnp.where(pivot, crossed, jnp.where(gone, 0.0, turned) - real * crossed + imag * weight)
        tiles[g] = tile
        within = place & 31
        gone = (within >= start) & (within < start + 8)
        rows = [(whole_row(tile, t), whole_row(turned, t)) for t in range(8)]
        for i, spreads in others.items():
            changes = [a * weight + b * crossed for (a, b), (weight, crossed) in zip(spreads, rows)]
            while len(changes) > 1:
                changes = [u + v for u, v in zip(changes[::2], changes[1::2])]
            tiles[i] = jnp.where(gone, 0.0, tiles[i]) - changes[0]
    return jnp.concatenate(tiles, axis=0)


def invert(z_ref):
    lane = lane_iota((LANES, LANES))
    sub = lax.broadcasted_iota(jnp.int32, (LANES, LANES), 0)
    for k in range(LANES // BLOCK):
        r = k * BLOCK
        p0, q0 = z_ref[0:128, 0:128], z_ref[0:128, 128:256]
        p1, q1 = z_ref[128:256, 0:128], z_ref[128:256, 128:256]
        zero = jnp.zeros_like(p0)
        first = jnp.where(lane < 32, turn(p0, -r), jnp.where(lane < 64, turn(q0, 32 - r), zero))
        second = jnp.where(lane < 64, zero, jnp.where(lane < 96, turn(p1, 64 - r), turn(q1, 96 - r)))
        diagonal = invert_block(first[r : r + 32] + second[r : r + 32])
        small = lane[0:32]
        left = jnp.concatenate(
            [jnp.where(small < 64, diagonal, 0.0), jnp.where(small < 64, 0.0, diagonal)], axis=0
        )

        def stacked(a, b, c, d):
            return jnp.concatenate(
                [
                    jnp.concatenate([a, b], axis=1),
                    jnp.concatenate([-b, a], axis=1),
                    jnp.concatenate([c, d], axis=1),
                    jnp.concatenate([-d, c], axis=1),
                ],
                axis=0,
            )

        rows = slice(r, r + 32)
        w = exact_dot(left, stacked(p0[rows], q0[rows], p1[rows], q1[rows]))
        here = (small >= r) & (small < r + 32)
        wp0 = jnp.where(here, turn(diagonal, r), w[0:32, 0:128])
        wq0 = jnp.where(here, turn(diagonal, r - 32), w[0:32, 128:256])
        wp1 = jnp.where(here, turn(diagonal, r - 64), w[32:64, 0:128])
        wq1 = jnp.where(here, turn(diagonal, r - 96), w[32:64, 128:256])
        inside = (sub >= r) & (sub < r + 32)
        first = jnp.where(inside, jnp.where(sub - r == lane, -1.0, 0.0), first)
        second = jnp.where(inside, jnp.where(sub - r == lane - 64, -1.0, 0.0), second)
        change = exact_dot(jnp.concatenate([first, second], axis=0), stacked(wp0, wq0, wp1, wq1))
        kept = inside | ((lane >= r) & (lane < r + 32))
        for j in range(2):
            for half in range(2):
                tile = (slice(j * 128, j * 128 + 128), slice(half * 128, half * 128 + 128))
                z_ref[tile] = jnp.where(kept, 0.0, z_ref[tile]) - change[tile]


def gather_fields(in_ref, fields, a):
    for q in range(4):
        for c in range(3):
            for group in range(2):
                vectors = swap_blocks(
                    in_ref[pl.ds((snap * 16 + group * 8) * 24 + a * 12 + c * 4 + q, 8, stride=24), :]
                    for snap in range(8)
                )
                for h in range(8):
                    fields[a, q, pl.ds(((c * 2 + group) * 8 + h) * 8, 8), :] = vectors[h]


def solve_kernel(ridge_ref, in_ref, out_ref, fields, gram, z):
    gather_fields(in_ref, fields, 0)
    owner = lax.axis_index("snap") * 16 + lax.axis_index("height")
    lane = lane_iota((LANES, LANES))
    sub = lax.broadcasted_iota(jnp.int32, (LANES, LANES), 0)
    diagonal = lane == sub
    large = []
    ridges = []
    for j in range(2):
        at = fields[0, 2 * j]
        bt = fields[0, 2 * j + 1]
        real = jnp.transpose(at)
        imag = jnp.transpose(bt)
        product = exact_dot(jnp.concatenate([real, imag], axis=0), jnp.concatenate([at, bt], axis=1))
        p = product[0:128, 0:128] + product[128:256, 128:256]
        q = product[128:256, 0:128] - product[0:128, 128:256]
        ridge = lax.shift_left(jnp.int32(LANES // 4), ridge_ref[j * LANES + owner]).astype(jnp.float32)
        ridges.append(ridge)
        rows = slice(j * 128, j * 128 + 128)
        gram[rows, 0:128] = p
        gram[rows, 128:256] = q
        z[rows, 0:128] = p + jnp.where(diagonal, ridge, 0.0)
        z[rows, 128:256] = q
        trace = jnp.sum(jnp.where(diagonal, p, 0.0))
        large.append(trace > ridge * float(LANES))
    gather_fields(in_ref, fields, 1)
    invert(z)
    misses = jnp.zeros((8, LANES), jnp.float32)
    energy = jnp.zeros((8, LANES), jnp.float32)
    for j in range(2):
        rows = slice(j * 128, j * 128 + 128)
        ridge = ridges[j]

        @pl.when(large[j])
        def _():
            z[rows, 0:128] = jnp.where(diagonal, 1.0, 0.0) - ridge * z[rows, 0:128]
            z[rows, 128:256] = -ridge * z[rows, 128:256]

        @pl.when(jnp.logical_not(large[j]))
        def _():
            p, q = gram[rows, 0:128], gram[rows, 128:256]
            full = jnp.concatenate(
                [jnp.concatenate([p, q], axis=1), jnp.concatenate([-q, p], axis=1)], axis=0
            )
            z[rows, :] = exact_dot(z[rows, :], full)

        tp, tq = z[rows, 0:128], z[rows, 128:256]
        target = jnp.concatenate([fields[1, 2 * j], fields[1, 2 * j + 1]], axis=1)
        mixing = jnp.concatenate(
            [jnp.concatenate([tp, tq], axis=1), jnp.concatenate([-tq, tp], axis=1)], axis=0
        )
        fitted = lax.dot_general(
            target,
            mixing,
            (((1,), (0,)), ((), ())),
            precision=lax.Precision.HIGH,
            preferred_element_type=jnp.float32,
        )
        missed = (target - fitted) ** 2
        square = target**2
        misses += jnp.sum((missed[:, 0:128] + missed[:, 128:256]).reshape(48, 8, LANES), axis=0)
        energy += jnp.sum((square[:, 0:128] + square[:, 128:256]).reshape(48, 8, LANES), axis=0)
        for r in range(2):
            for c in range(3):
                for group in range(2):
                    base = (c * 2 + group) * 64
                    vectors = swap_blocks(
                        fitted[base + h * 8 : base + h * 8 + 8, r * 128 : r * 128 + 128] for h in range(8)
                    )
                    for snap in range(8):
                        out_ref[
                            pl.ds((snap * 16 + group * 8) * 13 + c * 4 + 2 * j + r, 8, stride=13), :
                        ] = vectors[snap]
    row = lane_iota((8, LANES))
    sums = jnp.where(row == 0, jnp.sum(misses), jnp.where(row == 1, jnp.sum(energy), 0.0))
    for group in range(16):
        out_ref[pl.ds(group * 8 * 13 + 12, 8, stride=13), :] = sums


def spread_kernel(in_ref, out_ref, misfit_ref):
    for c in range(3):
        for q in range(4):
            tile = jnp.transpose(in_ref[pl.ds(c * 4 + q, LANES, stride=13), :])
            for s in range(16):
                out_ref[pl.ds(s * 96 + c * 32 + q, 8, stride=4), :] = tile[s * 8 : s * 8 + 8]
    sums = jnp.sum(in_ref[pl.ds(12, LANES, stride=13), :], axis=0, keepdims=True)
    lane = lane_iota((1, LANES))
    misses = jnp.sum(jnp.where(lane == 0, sums, 0.0))
    energy = jnp.sum(jnp.where(lane == 1, sums, 0.0))
    misfit_ref[...] = jnp.full((1, LANES), misses, jnp.float32) / jnp.full((1, LANES), energy, jnp.float32)


def vmem():
    return pl.BlockSpec(memory_space=pltpu.VMEM)


def params(megabytes, **more):
    return pltpu.CompilerParams(vmem_limit_bytes=megabytes * 1024 * 1024, **more)


def spectra(pairs, table, resolved, drain):
    block = pl.BlockSpec((16, 1, 256, LANES), lambda c: (0, c, 0, 0))
    whole = lambda shape: pl.BlockSpec(shape, lambda c: (0, 0))
    return pl.pallas_call(
        spectrum_kernel,
        grid=(3,),
        in_specs=[whole((2, 256)), whole((256, 256)), block, block],
        out_specs=whole((3072, LANES)),
        out_shape=jax.ShapeDtypeStruct((3072, LANES), jnp.float32),
        scratch_shapes=[
            pltpu.VMEM((512, 4096), jnp.bfloat16),
            pltpu.VMEM((128 * PITCH, LANES), jnp.float32),
            pltpu.VMEM((256, 4096), jnp.bfloat16),
        ],
        compiler_params=params(56, dimension_semantics=("arbitrary",)),
    )(pairs, table, resolved, drain)


def settle(ridge_index, arrived):
    return pl.pallas_call(
        solve_kernel,
        in_specs=[pl.BlockSpec(memory_space=pltpu.SMEM), vmem()],
        out_specs=vmem(),
        out_shape=jax.ShapeDtypeStruct((1664, LANES), jnp.float32),
        scratch_shapes=[
            pltpu.VMEM((2, 4, 384, LANES), jnp.float32),
            pltpu.VMEM((256, 256), jnp.float32),
            pltpu.VMEM((256, 256), jnp.float32),
        ],
        compiler_params=params(24),
    )(ridge_index, arrived)


def spread(returned):
    return pl.pallas_call(
        spread_kernel,
        in_specs=[vmem()],
        out_specs=(vmem(), vmem()),
        out_shape=(
            jax.ShapeDtypeStruct((1536, LANES), jnp.float32),
            jax.ShapeDtypeStruct((1, LANES), jnp.float32),
        ),
        compiler_params=params(24),
    )(returned)


def exchange(values, rows):
    moved = lax.all_to_all(
        values.reshape(128, 1, rows * LANES), ("snap", "height"), split_axis=0, concat_axis=0, tiled=True
    )
    return moved.reshape(128 * rows, LANES)


def per_device(resolved, drain, pair_list, ridge_index):
    table = twiddle_rows(resolved.shape[-1])
    pairs = pair_list.T
    sent = spectra(
        pairs, table, resolved.reshape(16, 3, 256, LANES), drain.reshape(16, 3, 256, LANES)
    )
    fitted = settle(ridge_index, exchange(sent, 24))
    predicted, misfit = spread(exchange(fitted, 13))
    predicted = predicted.reshape(16, 3, 8, 2, 2, 128).transpose(0, 1, 2, 4, 3, 5)
    return (predicted.reshape(16, 3, 8, 2, 256), misfit[0, 0:1])


def solution(mesh):
    return jax.shard_map(
        per_device,
        mesh=mesh,
        in_specs=(
            P("snap", None, "height", None, None, None),
            P("snap", None, "height", None, None, None),
            P(),
            P(),
        ),
        out_specs=(P("snap", None, "height", None, None), P()),
        check_vma=False,
    )
```

```python
import math

import jax
import jax.numpy as jnp
import numpy as np
from jax import lax
from jax.experimental import pallas as pl
from jax.experimental.pallas import tpu as pltpu
from jax.sharding import PartitionSpec as P

HIGHEST = lax.Precision.HIGHEST
BLOCK = 32
LANES = 128
PITCH = 33


def twiddle_rows(length):
    grid = np.arange(length)
    theta = ((grid[:, None] * grid[None, :]) % length) * (2.0 * math.pi / length)
    scaling = 1.0 / math.sqrt(length)
    cosine = np.cos(theta) * scaling
    sine = np.sin(theta) * scaling
    upper = np.concatenate([cosine, -sine], axis=1)
    lower = np.concatenate([sine, cosine], axis=1)
    table = np.concatenate([upper, lower], axis=0)
    return jnp.asarray(np.ascontiguousarray(table.T), dtype=jnp.bfloat16)


def lane_iota(shape):
    return lax.broadcasted_iota(jnp.int32, shape, len(shape) - 1)


def exact_dot(a, b):
    return lax.dot_general(
        a, b, (((1,), (0,)), ((), ())), precision=HIGHEST, preferred_element_type=jnp.float32
    )


def turn(values, amount):
    amount %= LANES
    return pltpu.roll(values, amount, 1) if amount else values


def swap_blocks(values):
    values = list(values)
    lane = lane_iota(values[0].shape)
    for bit in (1, 2, 4):
        odd = (lane & bit) != 0
        for index in range(8):
            if index & bit:
                continue
            low, high = values[index], values[index | bit]
            values[index] = jnp.where(odd, turn(high, bit), low)
            values[index | bit] = jnp.where(odd, high, turn(low, -bit))
    return values


def spectrum_kernel(pairs_ref, table_ref, x_ref, y_ref, out_ref, masked, wide, packed):
    component = pl.program_id(0)

    @pl.when(component == 0)
    def _():
        for j in range(2):
            lanes = pl.ds(j * LANES, LANES)
            mode = pairs_ref[0:1, lanes].astype(jnp.float32)
            wave = pairs_ref[1:2, lanes].astype(jnp.float32)
            mode = jnp.transpose(jnp.broadcast_to(mode, (LANES, LANES)))
            wave = jnp.transpose(jnp.broadcast_to(wave, (LANES, LANES)))
            chosen = wave == lane_iota((LANES, LANES)).astype(jnp.float32)
            chosen = jnp.where(chosen, 1.0, 0.0).astype(jnp.bfloat16)
            mode = jnp.concatenate([mode, mode], axis=1)
            for r in range(2):
                rows = jnp.dot(
                    chosen, table_ref[r * LANES : (r + 1) * LANES, :], preferred_element_type=jnp.float32
                ).astype(jnp.bfloat16)
                for m in range(16):
                    masked[pl.ds((j * 2 + r) * LANES, LANES), pl.ds(m * 256, 256)] = rows * jnp.where(
                        mode == float(m), 1.0, 0.0
                    ).astype(jnp.bfloat16)

    for a, ref in enumerate((x_ref, y_ref)):
        for group in range(128):
            first = group % 8 * 32
            wide[group * PITCH : group * PITCH + 32, :] = ref[group // 8, 0, first : first + 32, :].astype(
                jnp.float32
            )
        for part in range(32):
            packed[a * LANES : (a + 1) * LANES, pl.ds(part * LANES, LANES)] = wide[
                pl.ds(part, LANES, stride=PITCH), :
            ].astype(jnp.bfloat16)
    product = lax.dot_general(
        masked[...], packed[...], (((1,), (1,)), ((), ())), preferred_element_type=jnp.float32
    )
    for a in range(2):
        for q in range(4):
            for group in range(16):
                row = q * LANES + group * 8
                out_ref[pl.ds(group * 8 * 24 + a * 12 + component * 4 + q, 8, stride=24), :] = product[
                    row : row + 8, a * LANES : (a + 1) * LANES
                ]


def invert_block(block):
    count = BLOCK // 8
    lane = lane_iota((8, LANES))
    sub = lax.broadcasted_iota(jnp.int32, (8, LANES), 0)
    place = lane & 63
    second = lane >= 64

    def column(tile, t):
        def spread_lane(at):
            return jnp.broadcast_to(tile[:, at : at + 1], (8, LANES))

        return jnp.where(second, spread_lane(64 + t), spread_lane(t))

    def whole_row(tile, t):
        return jnp.broadcast_to(tile[t : t + 1, :], (8, LANES))

    tiles = [block[8 * i : 8 * i + 8] for i in range(count)]
    for g in range(count):
        start = 8 * g
        tile = tiles[g]
        turned = jnp.where(place < 32, -turn(tile, -32), turn(tile, 32))
        columns = [(column(tile, start + t), column(tile, start + t + 32)) for t in range(8)]
        others = {
            i: [(column(tiles[i], start + t), column(tiles[i], start + t + 32)) for t in range(8)]
            for i in range(count)
            if i != g
        }
        for t in range(8):
            real, imag = columns[t]
            pivot = sub == t
            inverse = 1.0 / whole_row(real, t)
            for later in range(t + 1, 8):
                other_real, other_imag = columns[later]
                scaled_real = whole_row(other_real, t) * inverse
                scaled_imag = whole_row(other_imag, t) * inverse
                columns[later] = (
                    jnp.where(pivot, scaled_real, other_real - real * scaled_real + imag * scaled_imag),
                    jnp.where(pivot, scaled_imag, other_imag - real * scaled_imag - imag * scaled_real),
                )
            at_real = place == start + t
            at_imag = place == start + t + 32
            gone = at_real | at_imag
            weight = jnp.where(at_real, inverse, jnp.where(at_imag, 0.0, whole_row(tile, t) * inverse))
            crossed = jnp.where(at_real, 0.0, jnp.where(at_imag, inverse, whole_row(turned, t) * inverse))
            tile = jnp.where(pivot, weight, jnp.where(gone, 0.0, tile) - real * weight - imag * crossed)
            turned = jnp.where(pivot, crossed, jnp.where(gone, 0.0, turned) - real * crossed + imag * weight)
        tiles[g] = tile
        within = place & 31
        gone = (within >= start) & (within < start + 8)
        rows = [(whole_row(tile, t), whole_row(turned, t)) for t in range(8)]
        for i, spreads in others.items():
            changes = [a * weight + b * crossed for (a, b), (weight, crossed) in zip(spreads, rows)]
            while len(changes) > 1:
                changes = [u + v for u, v in zip(changes[::2], changes[1::2])]
            tiles[i] = jnp.where(gone, 0.0, tiles[i]) - changes[0]
    return jnp.concatenate(tiles, axis=0)


def invert(z_ref):
    lane = lane_iota((LANES, LANES))
    sub = lax.broadcasted_iota(jnp.int32, (LANES, LANES), 0)
    for k in range(LANES // BLOCK):
        r = k * BLOCK
        p0, q0 = z_ref[0:128, 0:128], z_ref[0:128, 128:256]
        p1, q1 = z_ref[128:256, 0:128], z_ref[128:256, 128:256]
        zero = jnp.zeros_like(p0)
        first = jnp.where(lane < 32, turn(p0, -r), jnp.where(lane < 64, turn(q0, 32 - r), zero))
        second = jnp.where(lane < 64, zero, jnp.where(lane < 96, turn(p1, 64 - r), turn(q1, 96 - r)))
        diagonal = invert_block(first[r : r + 32] + second[r : r + 32])
        small = lane[0:32]
        left = jnp.concatenate(
            [jnp.where(small < 64, diagonal, 0.0), jnp.where(small < 64, 0.0, diagonal)], axis=0
        )

        def stacked(a, b, c, d):
            return jnp.concatenate(
                [
                    jnp.concatenate([a, b], axis=1),
                    jnp.concatenate([-b, a], axis=1),
                    jnp.concatenate([c, d], axis=1),
                    jnp.concatenate([-d, c], axis=1),
                ],
                axis=0,
            )

        rows = slice(r, r + 32)
        w = exact_dot(left, stacked(p0[rows], q0[rows], p1[rows], q1[rows]))
        here = (small >= r) & (small < r + 32)
        wp0 = jnp.where(here, turn(diagonal, r), w[0:32, 0:128])
        wq0 = jnp.where(here, turn(diagonal, r - 32), w[0:32, 128:256])
        wp1 = jnp.where(here, turn(diagonal, r - 64), w[32:64, 0:128])
        wq1 = jnp.where(here, turn(diagonal, r - 96), w[32:64, 128:256])
        inside = (sub >= r) & (sub < r + 32)
        first = jnp.where(inside, jnp.where(sub - r == lane, -1.0, 0.0), first)
        second = jnp.where(inside, jnp.where(sub - r == lane - 64, -1.0, 0.0), second)
        change = exact_dot(jnp.concatenate([first, second], axis=0), stacked(wp0, wq0, wp1, wq1))
        kept = inside | ((lane >= r) & (lane < r + 32))
        for j in range(2):
            for half in range(2):
                tile = (slice(j * 128, j * 128 + 128), slice(half * 128, half * 128 + 128))
                z_ref[tile] = jnp.where(kept, 0.0, z_ref[tile]) - change[tile]


def gather_fields(in_ref, fields, a):
    for q in range(4):
        for c in range(3):
            for group in range(2):
                vectors = swap_blocks(
                    in_ref[pl.ds((snap * 16 + group * 8) * 24 + a * 12 + c * 4 + q, 8, stride=24), :]
                    for snap in range(8)
                )
                for h in range(8):
                    fields[a, q, pl.ds(((c * 2 + group) * 8 + h) * 8, 8), :] = vectors[h]


def solve_kernel(ridge_ref, in_ref, out_ref, fields, gram, z):
    gather_fields(in_ref, fields, 0)
    owner = lax.axis_index("snap") * 16 + lax.axis_index("height")
    lane = lane_iota((LANES, LANES))
    sub = lax.broadcasted_iota(jnp.int32, (LANES, LANES), 0)
    diagonal = lane == sub
    large = []
    ridges = []
    for j in range(2):
        at = fields[0, 2 * j]
        bt = fields[0, 2 * j + 1]
        real = jnp.transpose(at)
        imag = jnp.transpose(bt)
        product = exact_dot(jnp.concatenate([real, imag], axis=0), jnp.concatenate([at, bt], axis=1))
        p = product[0:128, 0:128] + product[128:256, 128:256]
        q = product[128:256, 0:128] - product[0:128, 128:256]
        ridge = lax.shift_left(jnp.int32(LANES // 4), ridge_ref[j * LANES + owner]).astype(jnp.float32)
        ridges.append(ridge)
        rows = slice(j * 128, j * 128 + 128)
        gram[rows, 0:128] = p
        gram[rows, 128:256] = q
        z[rows, 0:128] = p + jnp.where(diagonal, ridge, 0.0)
        z[rows, 128:256] = q
        trace = jnp.sum(jnp.where(diagonal, p, 0.0))
        large.append(trace > ridge * float(LANES))
    gather_fields(in_ref, fields, 1)
    invert(z)
    misses = jnp.zeros((8, LANES), jnp.float32)
    energy = jnp.zeros((8, LANES), jnp.float32)
    for j in range(2):
        rows = slice(j * 128, j * 128 + 128)
        ridge = ridges[j]

        @pl.when(large[j])
        def _():
            z[rows, 0:128] = jnp.where(diagonal, 1.0, 0.0) - ridge * z[rows, 0:128]
            z[rows, 128:256] = -ridge * z[rows, 128:256]

        @pl.when(jnp.logical_not(large[j]))
        def _():
            p, q = gram[rows, 0:128], gram[rows, 128:256]
            full = jnp.concatenate(
                [jnp.concatenate([p, q], axis=1), jnp.concatenate([-q, p], axis=1)], axis=0
            )
            z[rows, :] = exact_dot(z[rows, :], full)

        tp, tq = z[rows, 0:128], z[rows, 128:256]
        target = jnp.concatenate([fields[1, 2 * j], fields[1, 2 * j + 1]], axis=1)
        mixing = jnp.concatenate(
            [jnp.concatenate([tp, tq], axis=1), jnp.concatenate([-tq, tp], axis=1)], axis=0
        )
        fitted = exact_dot(target, mixing)
        missed = (target - fitted) ** 2
        square = target**2
        misses += jnp.sum((missed[:, 0:128] + missed[:, 128:256]).reshape(48, 8, LANES), axis=0)
        energy += jnp.sum((square[:, 0:128] + square[:, 128:256]).reshape(48, 8, LANES), axis=0)
        for r in range(2):
            for c in range(3):
                for group in range(2):
                    base = (c * 2 + group) * 64
                    vectors = swap_blocks(
                        fitted[base + h * 8 : base + h * 8 + 8, r * 128 : r * 128 + 128] for h in range(8)
                    )
                    for snap in range(8):
                        out_ref[
                            pl.ds((snap * 16 + group * 8) * 13 + c * 4 + 2 * j + r, 8, stride=13), :
                        ] = vectors[snap]
    row = lane_iota((8, LANES))
    sums = jnp.where(row == 0, jnp.sum(misses), jnp.where(row == 1, jnp.sum(energy), 0.0))
    for group in range(16):
        out_ref[pl.ds(group * 8 * 13 + 12, 8, stride=13), :] = sums


def spread_kernel(in_ref, out_ref, misfit_ref):
    for c in range(3):
        for q in range(4):
            tile = jnp.transpose(in_ref[pl.ds(c * 4 + q, LANES, stride=13), :])
            for s in range(16):
                out_ref[pl.ds(s * 96 + c * 32 + q, 8, stride=4), :] = tile[s * 8 : s * 8 + 8]
    sums = jnp.sum(in_ref[pl.ds(12, LANES, stride=13), :], axis=0, keepdims=True)
    lane = lane_iota((1, LANES))
    misses = jnp.sum(jnp.where(lane == 0, sums, 0.0))
    energy = jnp.sum(jnp.where(lane == 1, sums, 0.0))
    misfit_ref[...] = jnp.full((1, LANES), misses, jnp.float32) / jnp.full((1, LANES), energy, jnp.float32)


def vmem():
    return pl.BlockSpec(memory_space=pltpu.VMEM)


def params(megabytes, **more):
    return pltpu.CompilerParams(vmem_limit_bytes=megabytes * 1024 * 1024, **more)


def spectra(pairs, table, resolved, drain):
    block = pl.BlockSpec((16, 1, 256, LANES), lambda c: (0, c, 0, 0))
    whole = lambda shape: pl.BlockSpec(shape, lambda c: (0, 0))
    return pl.pallas_call(
        spectrum_kernel,
        grid=(3,),
        in_specs=[whole((2, 256)), whole((256, 256)), block, block],
        out_specs=whole((3072, LANES)),
        out_shape=jax.ShapeDtypeStruct((3072, LANES), jnp.float32),
        scratch_shapes=[
            pltpu.VMEM((512, 4096), jnp.bfloat16),
            pltpu.VMEM((128 * PITCH, LANES), jnp.float32),
            pltpu.VMEM((256, 4096), jnp.bfloat16),
        ],
        compiler_params=params(56, dimension_semantics=("arbitrary",)),
    )(pairs, table, resolved, drain)


def settle(ridge_index, arrived):
    return pl.pallas_call(
        solve_kernel,
        in_specs=[pl.BlockSpec(memory_space=pltpu.SMEM), vmem()],
        out_specs=vmem(),
        out_shape=jax.ShapeDtypeStruct((1664, LANES), jnp.float32),
        scratch_shapes=[
            pltpu.VMEM((2, 4, 384, LANES), jnp.float32),
            pltpu.VMEM((256, 256), jnp.float32),
            pltpu.VMEM((256, 256), jnp.float32),
        ],
        compiler_params=params(24),
    )(ridge_index, arrived)


def spread(returned):
    return pl.pallas_call(
        spread_kernel,
        in_specs=[vmem()],
        out_specs=(vmem(), vmem()),
        out_shape=(
            jax.ShapeDtypeStruct((1536, LANES), jnp.float32),
            jax.ShapeDtypeStruct((1, LANES), jnp.float32),
        ),
        compiler_params=params(24),
    )(returned)


def exchange(values, rows):
    moved = lax.all_to_all(
        values.reshape(128, 1, rows * LANES), ("snap", "height"), split_axis=0, concat_axis=0, tiled=True
    )
    return moved.reshape(128 * rows, LANES)


def per_device(resolved, drain, pair_list, ridge_index):
    table = twiddle_rows(resolved.shape[-1])
    pairs = pair_list.T
    sent = spectra(
        pairs, table, resolved.reshape(16, 3, 256, LANES), drain.reshape(16, 3, 256, LANES)
    )
    fitted = settle(ridge_index, exchange(sent, 24))
    predicted, misfit = spread(exchange(fitted, 13))
    predicted = predicted.reshape(16, 3, 8, 2, 2, 128).transpose(0, 1, 2, 4, 3, 5)
    return (predicted.reshape(16, 3, 8, 2, 256), misfit[0, 0:1])


def solution(mesh):
    return jax.shard_map(
        per_device,
        mesh=mesh,
        in_specs=(
            P("snap", None, "height", None, None, None),
            P("snap", None, "height", None, None, None),
            P(),
            P(),
        ),
        out_specs=(P("snap", None, "height", None, None), P()),
        check_vma=False,
    )
```
